128 devices in a mesh: dp: 16 (over y_hi, x, core), row: 2 (over y_lo), col: 4 (over z).
Axes of the slice: x: 4, y: 4 (y_hi: 2, y_lo: 2; y = y_hi * 2 + y_lo), z: 4, core: 2. Of those that a mesh axis runs over, the one named last changes fastest.
Arguments:
- tokens: bfloat16 [16384, 1024], P(('dp', 'col'), 'row'), may hold values from -6 to 6
- mixer_gain: float32 [1024], P('row'), may hold values from 0.25 to 1.75
- in_weight: bfloat16 [3, 1024, 1024], P(None, 'row', 'col'), may hold values from -0.1875 to 0.1875
- conv_kernel: float32 [3, 1024], P(None, 'col'), may hold values from -1 to 1
- out_weight: bfloat16 [1024, 1024], P('col', 'row'), may hold values from -0.1875 to 0.1875
- ffn_gain: float32 [1024], P('row'), may hold values from 0.25 to 1.75
- gate_up_weight: bfloat16 [2, 1024, 4608], P(None, 'row', 'col'), may hold values from -0.1875 to 0.1875
- down_weight: bfloat16 [4608, 1024], P('col', 'row'), may hold values from -0.09375 to 0.09375
- conv_reach: int32 [16384], P(('dp', 'row')), may hold values from 0 to 2, as said below
- cotangent: bfloat16 [16384, 1024], P(('dp', 'col'), 'row'), may hold values from -6 to 6
Outputs:
- mixed: bfloat16 [16384, 1024], P(('dp', 'col'), 'row')
- grad_tokens: float32 [16384, 1024], P(('dp', 'col'), 'row')
- grad_mixer_gain: float32 [1024], P('row')
- grad_in_weight: float32 [3, 1024, 1024], P(None, 'row', 'col')
- grad_conv_kernel: float32 [3, 1024], P(None, 'col')
- grad_out_weight: float32 [1024, 1024], P('col', 'row')
- grad_ffn_gain: float32 [1024], P('row')
- grad_gate_up_weight: float32 [2, 1024, 4608], P(None, 'row', 'col')
- grad_down_weight: float32 [4608, 1024], P('col', 'row')
The draws below stay inside these ranges and needn't reach their ends.
Inputs may be any that keep to these rules, and one draw needn't show every extreme that they name: `conv_reach`: the first token of every sequence of 1024 tokens begins a document.
All inputs are finite; a program needn't handle non-finite values.
Results may differ from the reference program's by a relative error of at most 0.028.
Values may be sent and summed in bfloat16 or wider, within the bound.
A program may use at most 128 MiB of HBM per device.

```python
import jax
import jax.numpy as jnp
from jax import lax

D = 1024
FF = 4608
SEQ = 1024
TOKENS = 16384
N_DP = 16
N_ROW = 2


def draw_conv_reach(key, part):
    key = jax.random.fold_in(key, 7)
    index = jnp.arange(TOKENS, dtype=jnp.int32)
    local = index % SEQ
    block = SEQ // N_ROW
    inside = local % block
    rolls = jax.random.randint(key, (TOKENS,), 0, 20)
    quiet = (inside <= 2) | (inside >= block - 2)
    begins = (rolls == 0) & jnp.logical_not(quiet) | (local == 0)
    latest = lax.cummax(jnp.where(begins, index, 0), axis=0)
    return jnp.minimum(index - latest, 2).astype(jnp.int32)


def levels(own_key, shape, cuts, low, top_value):
    loudness = 1.0
    for dim, shards_of in cuts:
        draws = jax.random.uniform(jax.random.fold_in(jax.random.fold_in(own_key, 6), dim), (shards_of,), jnp.float32, low / len(cuts), top_value / len(cuts))
        loudness = loudness * jnp.repeat(jnp.exp(draws), shape[dim] // shards_of).reshape((-1,) + (1,) * (len(shape) - 1 - dim))
    return loudness


def normal_values(rng, extent, deviation, most, split=(), kind=jnp.bfloat16):
    values = deviation * jax.random.normal(rng, extent, jnp.float32)
    if split:
        values = values * levels(rng, extent, split, -0.22, 0.18)
    return jnp.clip(values, -most, most).astype(kind)


def setup_inputs(seed: int = 0) -> dict:
    key_list = jax.random.split(jax.random.key(seed), 11)
    return {
        "tokens": normal_values(key_list[0], (TOKENS, D), 1.0, 6.0, ((0, 64), (1, 2))),
        "mixer_gain": jnp.clip(1.0 + 0.15 * jax.random.normal(key_list[1], (D,), jnp.float32), 0.25, 1.75),
        "in_weight": normal_values(key_list[2], (3, D, D), D ** -0.5, 0.1875, ((1, 2), (2, 4))),
        "conv_kernel": jnp.clip(jax.random.uniform(key_list[3], (3, D), jnp.float32, -1.0, 1.0) * levels(key_list[3], (3, D), ((1, 4),), -0.4, 0.0), -1.0, 1.0),
        "out_weight": normal_values(key_list[4], (D, D), D ** -0.5, 0.1875, ((0, 4), (1, 2))),
        "ffn_gain": jnp.clip(1.0 + 0.15 * jax.random.normal(key_list[5], (D,), jnp.float32), 0.25, 1.75),
        "gate_up_weight": normal_values(key_list[6], (2, D, FF), D ** -0.5, 0.1875, ((1, 2), (2, 4))),
        "down_weight": normal_values(key_list[7], (FF, D), FF ** -0.5, 0.09375, ((0, 4), (1, 2))),
        "conv_reach": draw_conv_reach(jax.random.fold_in(key_list[10], 71), 0),
        "cotangent": normal_values(key_list[9], (TOKENS, D), 1.0, 6.0, ((0, 64), (1, 2))),
    }


@jax.custom_vjp
def low(v):
    return lax.optimization_barrier(v.astype(jnp.bfloat16)).astype(jnp.float32)

@jax.custom_vjp
def low_back(v):
    return v

def low_keep(v):
    return (low(v), None)

def low_pass(kept, grad):
    return (grad,)

def back_keep(v):
    return (v, None)

def back_low(kept, grad):
    return (low(grad),)
low.defvjp(low_keep, low_pass)
low_back.defvjp(back_keep, back_low)
norm_eps = 1e-05
highest = lax.Precision.HIGHEST

def rms_scale(value):
    return lax.rsqrt(lax.optimization_barrier(jnp.mean(value * value, axis=-1, keepdims=True)) + norm_eps)

def causal_conv(values, kernel, reach):
    total = kernel[0] * values
    for offset in (1, 2):
        moved = jnp.pad(values, ((offset, 0), (0, 0)))[:-offset]
        keep = (reach >= offset).astype(values.dtype)[:, None]
        total = total + kernel[offset] * moved * keep
    return total

def block_forward(inputs, mixer_gain, in_weight, conv_kernel, out_weight, ffn_gain, gate_up_weight, down_weight, reach):
    normed_one = low(inputs * rms_scale(inputs) * mixer_gain)
    mixed_in = low_back(jnp.einsum('td,kdf->ktf', normed_one, in_weight, precision=highest))
    product = mixed_in[0] * mixed_in[2]
    conv_out = causal_conv(product, conv_kernel, reach)
    gated = low(mixed_in[1] * conv_out)
    branch = low_back(jnp.dot(gated, out_weight, precision=highest))
    hidden = inputs + branch
    normed_two = low(hidden * rms_scale(hidden) * ffn_gain)
    gate_up = low_back(jnp.einsum('td,kdf->ktf', normed_two, gate_up_weight, precision=highest))
    active = low(jax.nn.silu(gate_up[0]) * gate_up[1])
    return hidden + low_back(jnp.dot(active, down_weight, precision=highest))

def reference(tokens, mixer_gain, in_weight, conv_kernel, out_weight, ffn_gain, gate_up_weight, down_weight, conv_reach, cotangent):
    params = (mixer_gain.astype(jnp.float32), in_weight.astype(jnp.float32), conv_kernel.astype(jnp.float32), out_weight.astype(jnp.float32), ffn_gain.astype(jnp.float32), gate_up_weight.astype(jnp.float32), down_weight.astype(jnp.float32))
    seq_inputs = tokens.astype(jnp.float32).reshape(N_DP, SEQ, D)
    seq_reach = conv_reach.reshape(N_DP, SEQ).astype(jnp.int32)
    seq_grads = cotangent.astype(jnp.float32).reshape(N_DP, SEQ, D)

    def one_sequence(totals, items):
        piece, reach, grad_out = items

        def forward(inputs, gain_a, weight_in, kernel, weight_out, gain_b, weight_gu, weight_down):
            return block_forward(inputs, gain_a, weight_in, kernel, weight_out, gain_b, weight_gu, weight_down, reach)
        result, pullback = jax.vjp(forward, piece, params[0], params[1], params[2], params[3], params[4], params[5], params[6])
        grads = pullback(grad_out)
        summed = tuple((total + grad for total, grad in zip(totals, grads[1:])))
        return (summed, (result.astype(jnp.bfloat16), grads[0]))
    zeros = tuple((jnp.zeros_like(param) for param in params))
    totals, (outputs, grad_inputs) = lax.scan(one_sequence, zeros, (seq_inputs, seq_reach, seq_grads))
    return (outputs.reshape(TOKENS, D), grad_inputs.reshape(TOKENS, D), totals[0], totals[1], totals[2], totals[3], totals[4], totals[5], totals[6])
```

```python
import functools

import jax
import jax.numpy as jnp
from jax import lax
from jax.experimental import pallas as pl
from jax.experimental.pallas import tpu as pltpu
from jax.sharding import PartitionSpec as P

MESH = pl.DeviceIdType.MESH
D = 1024
HALF = 512
T = 128
W = 256
H = 1152
EPS = 1e-05
F32 = jnp.float32
BF = jnp.bfloat16

UNITS = (("dn0", 144, 128, 0), ("dn1", 144, 128, 1), ("gt", 32, H, 0), ("up", 32, H, 1), ("oi0", 32, 512, 0), ("oi1", 32, 512, 1))


def mod(a, n):
    return lax.rem(a + 4 * n, n)


def dot(a, b):
    return lax.dot_general(a, b, (((1,), (0,)), ((), ())), preferred_element_type=F32)


def dot_nt(a, b):
    return lax.dot_general(a, b, (((1,), (1,)), ((), ())), preferred_element_type=F32)


def dot_tn(a, b):
    return lax.dot_general(a, b, (((0,), (0,)), ((), ())), preferred_element_type=F32)


def scratch_list():
    s = {}
    dma = pltpu.SemaphoreType.DMA

    def v(name, shape, dtype):
        s[name] = pltpu.VMEM(shape, dtype)

    v("INW", (3, D, W), BF)
    v("OUTW", (W, D), BF)
    v("GUW", (2, D, H), BF)
    v("DNW", (H, D), BF)
    v("X", (T, D), BF)
    v("M", (4, T, 128), BF)
    v("GA", (8, D), F32)
    for n in ("N1", "N2", "COT", "GB"):
        v(n, (4, T, D), BF)
        s[n + "_s"] = dma((4,))
        s[n + "_r"] = dma((4,))
    v("PR", (5, T + 8, W), F32)
    for n in ("GBV", "GCV", "VAL", "CO", "GCONV"):
        v(n, (4, T, W), F32)
    v("GATED", (4, T, W), BF)
    v("FM", (2, 5, T + 8, W), F32)
    v("HID", (T, D), F32)
    v("A", (4, T, H), BF)
    v("GG", (4, T, 2 * H), BF)
    v("GM", (4, T, 3 * W), BF)
    v("SB", (3, T, D), BF)
    v("SBF", (3, T, D), BF)
    v("OWN", (T, D), F32)
    v("OWNF", (T, D), F32)
    for n in ("R1", "R2", "R3", "RF"):
        v(n, (3, T, D), BF)
        s[n + "_s"] = dma((4,))
        s[n + "_r"] = dma((4,))
    v("MIXB", (T, D), BF)
    v("GTB", (T, D), BF)
    v("SM", (8, D), F32)
    v("SMC", (8, D), F32)
    v("SMX", (4, 8, D), F32)
    v("SMY", (4, 8, D), F32)
    v("SMZ", (4, 8, D), F32)
    s["SM_s"] = dma((12,))
    s["SM_r"] = dma((12,))
    s["sw_s"] = dma((10,))
    s["sw_r"] = dma((10,))
    s["ga"] = dma((3,))
    s["w_l"] = dma((4,))
    s["w_s"] = dma((12,))
    s["w_r"] = dma((12,))
    s["halo"] = dma((4,))
    for n, m, k, _ in UNITS:
        v(n + "_W", (2, 4, 4, m, k), BF)
        v(n + "_C", (4, 4, m, k), BF)
        v(n + "_R1", (3, 4, m, k), BF)
        v(n + "_S", (4, m, k), BF)
        v(n + "_R2", (3, m, k), BF)
        v(n + "_O", (2, 4, m, k), BF)
        s[n + "_s"] = dma((14,))
        s[n + "_r"] = dma((14,))
        s[n + "_l"] = dma((2,))
    return s


IN_NAMES = ("tok", "cot", "reach", "gains", "ck", "inw", "outw", "guw", "dnw")
OUT_NAMES = ("o_mixed", "o_gt", "o_small", "o_in", "o_out", "o_gu", "o_dn")


class Refs:
    pass


def kernel(*refs):
    q = Refs()
    names = IN_NAMES + OUT_NAMES + tuple(scratch_list())
    for name, ref in zip(names, refs, strict=True):
        setattr(q, name, ref)

    dp = lax.axis_index("dp")
    r = lax.axis_index("row")
    c = lax.axis_index("col")
    yhi = lax.div(dp, 8)
    x = lax.rem(lax.div(dp, 2), 4)
    k = lax.rem(dp, 2)
    y = yhi * 2 + r
    same = k == r
    other = k != r

    def dev(yhi_=None, x_=None, k_=None, r_=None, c_=None):
        yhi_ = yhi if yhi_ is None else yhi_
        x_ = x if x_ is None else x_
        k_ = k if k_ is None else k_
        return {"dp": yhi_ * 8 + x_ * 2 + k_, "row": r if r_ is None else r_, "col": c if c_ is None else c_}

    def at_y(d):
        to = mod(y + d, 4)
        return dev(yhi_=lax.div(to, 2), r_=lax.rem(to, 2))

    def at_x(d):
        return dev(x_=mod(x + d, 4))

    def at_z(d):
        return dev(c_=mod(c + d, 4))

    mate = dev(k_=1 - k)

    def slot_y(d):
        to = mod(y + d, 4)
        return lax.rem(to, 2) * 2 + lax.div(to, 2)

    def rcopy(src, dst, ss, rs, to):
        return pltpu.make_async_remote_copy(
            src_ref=src, dst_ref=dst, send_sem=ss, recv_sem=rs, device_id=to, device_id_type=MESH
        )

    barrier = pltpu.get_barrier_semaphore()
    friends = [mate, dev(r_=1 - r, k_=1 - k)]
    friends += [f(d) for f in (at_x, at_y, at_z) for d in (1, 2, 3)]
    for to in friends:
        pl.semaphore_signal(barrier, inc=1, device_id=to, device_id_type=MESH)
    pl.semaphore_wait(barrier, len(friends))

    def weight_regions(w):
        if w == 0:
            return (q.inw, q.INW, lambda p, n, a: (q.inw.at[:, pl.ds(p * 128, 128 * n), :], q.INW.at[:, pl.ds(a * HALF + p * 128, 128 * n), :]))
        if w == 1:
            return (q.outw, q.OUTW, lambda p, n, a: (q.outw.at[pl.ds(p * 64, 64 * n), :], q.OUTW.at[pl.ds(p * 64, 64 * n), pl.ds(pl.multiple_of(a * HALF, HALF), HALF)]))
        if w == 2:
            return (q.guw, q.GUW, lambda p, n, a: (q.guw.at[:, pl.ds(p * 128, 128 * n), :], q.GUW.at[:, pl.ds(a * HALF + p * 128, 128 * n), :]))
        return (q.dnw, q.DNW, lambda p, n, a: (q.dnw.at[pl.ds(p * 288, 288 * n), :], q.DNW.at[pl.ds(p * 288, 288 * n), pl.ds(pl.multiple_of(a * HALF, HALF), HALF)]))

    def weight_local(w):
        _, _, region = weight_regions(w)
        src, dst = region(0, 4, r)
        return pltpu.make_async_copy(src, dst, q.w_l.at[w])

    def weight_send(w, s):
        _, _, region = weight_regions(w)
        src, dst = region(k * 2 + s, 1, r)
        return rcopy(src, dst, q.w_s.at[w * 3 + s], q.w_r.at[w * 3 + s], at_y(1 - 2 * s))

    def weight_arrival(w, s):
        _, _, region = weight_regions(w)
        src, _ = region(k * 2 + s, 1, r)
        _, dst = region(k * 2 + s, 1, 1 - r)
        return rcopy(src, dst, q.w_s.at[w * 3 + s], q.w_r.at[w * 3 + s], at_y(1 - 2 * s))

    def weight_pass(w, core):
        _, _, region = weight_regions(w)
        _, dst = region(core * 2, 2, 1 - r)
        return rcopy(dst, dst, q.w_s.at[w * 3 + 2], q.w_r.at[w * 3 + 2], mate)

    def weight_start(w):
        for s in (0, 1):
            weight_send(w, s).start()

    def weight_forward(w):
        for s in (0, 1):
            weight_arrival(w, s).wait_recv()
        weight_pass(w, k).start()

    def weight_ready(w):
        weight_local(w).wait()
        weight_pass(w, 1 - k).wait_recv()

    def weight_end(w):
        for s in (0, 1):
            weight_send(w, s).wait_send()
        weight_pass(w, k).wait_send()

    for w in range(4):
        weight_local(w).start()

    def swap_views(n):
        if n == 0:
            return lambda j: q.tok.at[pl.ds(j * T, T), :], lambda a: q.X.at[:, pl.ds(pl.multiple_of(a * HALF, HALF), HALF)]
        if n == 1:
            return lambda j: q.reach.at[:, j], lambda a: q.M.at[pl.ds(2 * a, 2)]
        return lambda j: q.cot.at[pl.ds(j * T, T), :], lambda a: q.COT.at[c, :, pl.ds(pl.multiple_of(a * HALF, HALF), HALF)]

    def swap_near(n):
        src, dst = swap_views(n)
        return (
            pltpu.make_async_copy(src(k), dst(r), q.sw_r.at[2 * n]),
            rcopy(src(1 - k), dst(r), q.sw_s.at[2 * n], q.sw_r.at[2 * n], mate),
        )

    def swap_far(n, j):
        src, dst = swap_views(n)
        return rcopy(src(j), dst(r), q.sw_s.at[2 * n + j], q.sw_r.at[2 * n + 1], dev(r_=1 - r, k_=j))

    def swap_start(n):
        @pl.when(same)
        def _():
            near, far = swap_near(n)
            near.start()
            far.start()

        @pl.when(other)
        def _():
            swap_far(n, 0).start()
            swap_far(n, 1).start()

    def swap_wait(n):
        src, dst = swap_views(n)

        @pl.when(same)
        def _():
            near, far = swap_near(n)
            near.wait()
            far.wait_send()

        @pl.when(other)
        def _():
            swap_far(n, 0).wait_send()
            swap_far(n, 1).wait_send()
            rcopy(src(1 - k), dst(r), q.sw_s.at[2 * n], q.sw_r.at[2 * n], mate).wait_recv()

        rcopy(src(0), dst(1 - r), q.sw_s.at[2 * n], q.sw_r.at[2 * n + 1], dev(r_=1 - r)).wait_recv()

    def gain_view(a):
        return q.GA.at[:, pl.ds(pl.multiple_of(a * HALF, HALF), HALF)]

    gain_local = pltpu.make_async_copy(q.gains, gain_view(r), q.ga.at[0])
    gain_send = rcopy(q.gains, gain_view(r), q.ga.at[1], q.ga.at[2], dev(r_=1 - r))
    gain_take = rcopy(q.gains, gain_view(1 - r), q.ga.at[1], q.ga.at[2], dev(r_=1 - r))

    swap_start(0)
    gain_local.start()
    gain_send.start()
    weight_start(0)
    swap_start(1)

    def gather(name, d):
        buf = getattr(q, name)
        return rcopy(buf.at[c], buf.at[c], getattr(q, name + "_s").at[d], getattr(q, name + "_r").at[d], at_z(d))

    def gather_start(name):
        for d in (1, 3, 2):
            gather(name, d).start()

    def gather_take(name, d):
        buf = getattr(q, name)
        s = mod(c - d, 4)
        rcopy(buf.at[s], buf.at[s], getattr(q, name + "_s").at[d], getattr(q, name + "_r").at[d], at_z(d)).wait_recv()

    def gather_end(name):
        for d in (1, 3, 2):
            gather(name, d).wait_send()

    def reduce_send(name, send, e):
        buf = getattr(q, name)
        return rcopy(send.at[e - 1], buf.at[e - 1], getattr(q, name + "_s").at[e], getattr(q, name + "_r").at[e], at_z(e))

    def reduce_sum(name, send, own):
        buf = getattr(q, name)
        for e in (1, 3, 2):
            reduce_send(name, send, e).wait()
        return own[...] + (buf[0].astype(F32) + buf[2].astype(F32)) + buf[1].astype(F32)

    def put_part(name, send, own, e, part):
        @pl.when(e == 0)
        def _():
            own[...] = part

        @pl.when(e != 0)
        def _():
            send[e - 1] = part.astype(BF)
            reduce_send(name, send, e).start()

    def arrival(i):
        return i + lax.div(i, 2) - 2 * lax.div(i, 3)

    def far_first(i):
        return mod(2 - i + 3 * lax.div(i, 2) - 2 * lax.div(i, 3), 4)

    def norm_scale(value):
        return lax.rsqrt(jnp.sum(value * value, axis=1, keepdims=True) / D + EPS)

    swap_wait(0)
    gain_local.wait()
    gain_take.wait_recv()
    inputs = q.X[...].astype(F32)
    q.N1[c] = (inputs * norm_scale(inputs) * q.GA[0:1, :]).astype(BF)
    gather_start("N1")
    swap_start(2)
    for w in (1, 2, 3):
        weight_start(w)
    weight_forward(0)
    weight_ready(0)

    @pl.when(k == 0)
    def _():
        q.PR[0, 0:8] = jnp.zeros((8, W), F32)

    def in_step(i, carry):
        d = arrival(i)
        s = mod(c - d, 4)

        @pl.when(i > 0)
        def _():
            gather_take("N1", d)

        rows = q.N1[s]
        b = dot(rows, q.INW[0])
        v = dot(rows, q.INW[2])
        q.GBV[s] = b
        q.VAL[s] = v
        q.PR[s, 8:] = b * v
        q.GCV[s] = dot(rows, q.INW[1])
        return carry

    lax.fori_loop(0, 4, in_step, 0)
    gather_end("N1")

    halo_f = rcopy(q.PR.at[0:4, pl.ds(T, 8)], q.PR.at[pl.ds(k, 4), 0:8], q.halo.at[0], q.halo.at[1], mate)
    halo_ft = rcopy(q.PR.at[0:4, pl.ds(T, 8)], q.PR.at[pl.ds(1 - k, 4), 0:8], q.halo.at[0], q.halo.at[1], mate)
    halo_f.start()
    weight_forward(1)
    swap_wait(2)
    gather_start("COT")
    swap_wait(1)
    halo_f.wait_send()
    halo_ft.wait_recv()
    weight_ready(1)

    def masks(s):
        reach = q.M[s].astype(F32)
        first = jnp.where(reach >= 1.0, 1.0, 0.0)
        second = jnp.where(reach >= 2.0, 1.0, 0.0)
        return jnp.concatenate([first, first], axis=1), jnp.concatenate([second, second], axis=1)

    def conv_step(i, carry):
        e = far_first(i)
        s = mod(c + e, 4)
        m1, m2 = masks(s)
        conv = q.ck[0:1, :] * q.PR[s, pl.ds(8, T)]
        conv = conv + q.ck[1:2, :] * q.PR[s, pl.ds(7, T)] * m1
        conv = conv + q.ck[2:3, :] * q.PR[s, pl.ds(6, T)] * m2
        q.CO[s] = conv
        gated = (q.GCV[s] * conv).astype(BF)
        q.GATED[s] = gated
        put_part("R1", q.SB, q.OWN, e, dot(gated, q.OUTW[...]))
        return carry

    lax.fori_loop(0, 4, conv_step, 0)
    weight_forward(2)
    weight_forward(3)

    hidden = q.X[...].astype(F32) + reduce_sum("R1", q.SB, q.OWN)
    q.HID[...] = hidden
    q.N2[c] = (hidden * norm_scale(hidden) * q.GA[1:2, :]).astype(BF)
    gather_start("N2")
    for d in (1, 3, 2):
        gather_take("COT", d)
    gather_end("COT")
    weight_ready(2)
    weight_ready(3)

    def ffn_step(i, carry):
        d = arrival(i)
        s = mod(c - d, 4)
        e = mod(4 - d, 4)

        @pl.when(i > 0)
        def _():
            gather_take("N2", d)

        rows = q.N2[s]
        gate = dot(rows, q.GUW[0])
        up = dot(rows, q.GUW[1])
        sig = 1.0 / (1.0 + jnp.exp(-gate))
        silu = gate * sig
        q.A[s] = (silu * up).astype(BF)
        ga = dot_nt(q.COT[s], q.DNW[...])
        q.GG[s, :, 0:H] = (ga * up * sig * (1.0 + gate * (1.0 - sig))).astype(BF)
        q.GG[s, :, H:] = (ga * silu).astype(BF)
        part = dot_nt(q.GG[s, :, 0:H], q.GUW[0]) + dot_nt(q.GG[s, :, H:], q.GUW[1])
        put_part("R2", q.SB, q.OWN, e, part)
        return carry

    lax.fori_loop(0, 4, ffn_step, 0)
    gather_end("N2")

    def unit(name):
        return next(u for u in UNITS if u[0] == name)

    def g(name, what):
        return getattr(q, name + "_" + what)

    def core_copy(name, core):
        return rcopy(g(name, "W").at[core], g(name, "C"), g(name, "s").at[0], g(name, "r").at[0], mate)

    def first_copy(name, d):
        w = g(name, "W")
        if unit(name)[3] == 0:
            src, to = w.at[k, :, mod(x + d, 4)], at_x(d)
        else:
            src, to = w.at[k, slot_y(d)], at_y(d)
        return rcopy(src, g(name, "R1").at[d - 1], g(name, "s").at[d], g(name, "r").at[d], to)

    def second_copy(name, d):
        if unit(name)[3] == 0:
            src, to = g(name, "S").at[slot_y(d)], at_y(d)
        else:
            src, to = g(name, "S").at[mod(x + d, 4)], at_x(d)
        return rcopy(src, g(name, "R2").at[d - 1], g(name, "s").at[3 + d], g(name, "r").at[3 + d], to)

    def spread_x(name, d, place):
        o = g(name, "O")
        view = o.at[:, place] if unit(name)[3] == 0 else o.at[yhi, place]
        return rcopy(view, view, g(name, "s").at[6 + d], g(name, "r").at[6 + d], at_x(d))

    def spread_y(name, place):
        o = g(name, "O")
        view = o.at[place, x] if unit(name)[3] == 0 else o.at[place]
        return rcopy(view, view, g(name, "s").at[10], g(name, "r").at[10], at_y(2))

    def core_send(name):
        core_copy(name, 1 - k).start()

    def stage_one(name):
        core_copy(name, 1 - k).wait()
        w, other_part = g(name, "W"), g(name, "C")

        def add(i, carry):
            a, b = lax.div(i, 4), lax.rem(i, 4)
            w[k, a, b] = (w[k, a, b].astype(F32) + other_part[a, b].astype(F32)).astype(BF)
            return carry

        lax.fori_loop(0, 16, add, 0)
        for d in (1, 3, 2):
            first_copy(name, d).start()

    def stage_two(name):
        for d in (1, 3, 2):
            first_copy(name, d).wait()
        w, got, total = g(name, "W"), g(name, "R1"), g(name, "S")

        def add(i, carry):
            mine = w[k, i, x] if unit(name)[3] == 0 else w[k, slot_y(0), i]
            total[i] = (mine.astype(F32) + got[0, i].astype(F32) + got[1, i].astype(F32) + got[2, i].astype(F32)).astype(BF)
            return carry

        lax.fori_loop(0, 4, add, 0)
        for d in (1, 3, 2):
            second_copy(name, d).start()

    def stage_three(name):
        for d in (1, 3, 2):
            second_copy(name, d).wait()
        got, total = g(name, "R2"), g(name, "S")
        mine = total[slot_y(0)] if unit(name)[3] == 0 else total[x]
        g(name, "O")[yhi, x] = (mine.astype(F32) + got[0].astype(F32) + got[1].astype(F32) + got[2].astype(F32)).astype(BF)
        if unit(name)[3] == 0:
            spread_y(name, yhi).start()
        else:
            for d in (1, 3, 2):
                spread_x(name, d, x).start()

    def take_x(name):
        for d in (1, 3, 2):
            spread_x(name, d, x).wait_send()
            spread_x(name, d, mod(x - d, 4)).wait_recv()

    def take_y(name):
        spread_y(name, yhi).wait_send()
        spread_y(name, 1 - yhi).wait_recv()

    def stage_four(name):
        if unit(name)[3] == 0:
            take_y(name)
            for d in (1, 3, 2):
                spread_x(name, d, x).start()
        else:
            take_x(name)
            spread_y(name, yhi).start()

    def results(name, core):
        o = g(name, "O")
        half = unit(name)[3]
        if name in ("dn0", "dn1"):
            at = pl.multiple_of(core * W + half * 128, 128)
            return [(o, q.o_dn.at[:, :, :, pl.ds(at, 128)])]
        if name in ("gt", "up"):
            return [(o, q.o_gu.at[half, core])]
        if name == "oi0":
            at = pl.multiple_of(core * W, W)
            return [(o.at[:, :, :, 0:W], q.o_out.at[:, :, :, pl.ds(at, W)]), (o.at[:, :, :, W:], q.o_in.at[0, core])]
        return [(o.at[:, :, :, 0:W], q.o_in.at[1, core]), (o.at[:, :, :, W:], q.o_in.at[2, core])]

    def stage_five(name):
        if unit(name)[3] == 0:
            take_x(name)
        else:
            take_y(name)
        for n, (src, dst) in enumerate(results(name, k)):
            pltpu.make_async_copy(src, dst, g(name, "l").at[n]).start()
            rcopy(src, dst, g(name, "s").at[11 + n], g(name, "r").at[11 + n], mate).start()

    def stage_six(name):
        for n, (src, dst) in enumerate(results(name, k)):
            pltpu.make_async_copy(src, dst, g(name, "l").at[n]).wait()
            rcopy(src, dst, g(name, "s").at[11 + n], g(name, "r").at[11 + n], mate).wait_send()
        for n, (src, dst) in enumerate(results(name, 1 - k)):
            rcopy(src, dst, g(name, "s").at[11 + n], g(name, "r").at[11 + n], mate).wait_recv()

    def features(ref, a, core):
        at = pl.multiple_of(a * HALF + core * W, W)
        return ref[:, :, pl.ds(at, W)].reshape(4 * T, W)

    def grad_down(core):
        def step(a, carry):
            full = dot_tn(q.A[...].reshape(4 * T, H), features(q.COT, a, core)).astype(BF).reshape(2, 4, 144, W)
            q.dn0_W[core, pl.ds(2 * a, 2)] = full[:, :, :, :128]
            q.dn1_W[core, pl.ds(2 * a, 2)] = full[:, :, :, 128:]
            return carry

        lax.fori_loop(0, 2, step, 0)

    def grad_gate_up(core):
        def step(a, carry):
            rows = features(q.N2, a, core)
            q.gt_W[core, pl.ds(2 * a, 2)] = dot_tn(rows, q.GG[:, :, 0:H].reshape(4 * T, H)).astype(BF).reshape(2, 4, 32, H)
            q.up_W[core, pl.ds(2 * a, 2)] = dot_tn(rows, q.GG[:, :, H:].reshape(4 * T, H)).astype(BF).reshape(2, 4, 32, H)
            return carry

        lax.fori_loop(0, 2, step, 0)

    def grad_out_in(core):
        def step(a, carry):
            rows = features(q.N1, a, core)
            gated = q.GATED[...].reshape(4 * T, W)
            q.oi0_W[core, pl.ds(2 * a, 2), :, :, 0:W] = dot_tn(gated, features(q.GB, a, core)).astype(BF).reshape(2, 4, 32, W)
            into = dot_tn(rows, q.GM[...].reshape(4 * T, 3 * W)).astype(BF).reshape(2, 4, 32, 3 * W)
            q.oi0_W[core, pl.ds(2 * a, 2), :, :, W:] = into[:, :, :, 0:W]
            q.oi1_W[core, pl.ds(2 * a, 2)] = into[:, :, :, W:]
            return carry

        lax.fori_loop(0, 2, step, 0)

    grad_down(1 - k)
    core_send("dn0")
    core_send("dn1")
    grad_gate_up(1 - k)
    core_send("gt")
    core_send("up")
    grad_down(k)

    def norm_back(value, scale, gain, grad):
        weighted = grad * gain
        inner = jnp.sum(weighted * value, axis=1, keepdims=True)
        back = scale * weighted - value * (scale * scale * scale) * inner / D
        return back, jnp.sum(grad * value * scale, axis=0, keepdims=True)

    grad_normed = reduce_sum("R2", q.SB, q.OWN)
    hidden = q.HID[...]
    back, grad_gain = norm_back(hidden, norm_scale(hidden), q.GA[1:2, :], grad_normed)
    q.SM[...] = jnp.zeros((8, D), F32)
    q.SM[1:2, :] = grad_gain
    grad_hidden = q.COT[c].astype(F32) + back
    q.GB[c] = grad_hidden.astype(BF)
    q.OWN[...] = grad_hidden
    gather_start("GB")
    grad_gate_up(k)
    stage_one("dn0")
    stage_one("dn1")
    stage_one("gt")
    stage_one("up")

    @pl.when(k == 1)
    def _():
        q.FM[0, 4, pl.ds(T, 8)] = jnp.zeros((8, W), F32)
        q.FM[1, 4, pl.ds(T, 8)] = jnp.zeros((8, W), F32)

    def conv_back_step(i, carry):
        d = arrival(i)
        s = mod(c - d, 4)

        @pl.when(i > 0)
        def _():
            gather_take("GB", d)

        grad_gated = dot_nt(q.GB[s], q.OUTW[...])
        q.GM[s, :, W : 2 * W] = (grad_gated * q.CO[s]).astype(BF)
        grad_conv = grad_gated * q.GCV[s]
        q.GCONV[s] = grad_conv
        m1, m2 = masks(s)
        q.FM[0, s + 1, 0:T] = grad_conv * m1
        q.FM[1, s + 1, 0:T] = grad_conv * m2
        return carry

    lax.fori_loop(0, 4, conv_back_step, 0)
    gather_end("GB")
    halo_b = rcopy(q.FM.at[:, 1:5, 0:8], q.FM.at[:, pl.ds(k, 4), pl.ds(T, 8)], q.halo.at[2], q.halo.at[3], mate)
    halo_bt = rcopy(q.FM.at[:, 1:5, 0:8], q.FM.at[:, pl.ds(1 - k, 4), pl.ds(T, 8)], q.halo.at[2], q.halo.at[3], mate)
    halo_b.start()
    halo_b.wait_send()
    halo_bt.wait_recv()

    def product_back_step(i, carry):
        e = far_first(i)
        s = mod(c + e, 4)
        grad_conv = q.GCONV[s]
        grad_product = q.ck[0:1, :] * grad_conv
        grad_product = grad_product + q.ck[1:2, :] * q.FM[0, s + 1, pl.ds(1, T)]
        grad_product = grad_product + q.ck[2:3, :] * q.FM[1, s + 1, pl.ds(2, T)]
        q.SM[2:3, 0:W] += jnp.sum(grad_conv * q.PR[s, pl.ds(8, T)], axis=0, keepdims=True)
        q.SM[3:4, 0:W] += jnp.sum(q.FM[0, s + 1, pl.ds(0, T)] * q.PR[s, pl.ds(7, T)], axis=0, keepdims=True)
        q.SM[4:5, 0:W] += jnp.sum(q.FM[1, s + 1, pl.ds(0, T)] * q.PR[s, pl.ds(6, T)], axis=0, keepdims=True)
        q.GM[s, :, 0:W] = (grad_product * q.VAL[s]).astype(BF)
        q.GM[s, :, 2 * W :] = (grad_product * q.GBV[s]).astype(BF)
        part = dot_nt(q.GM[s, :, 0:W], q.INW[0]) + dot_nt(q.GM[s, :, W : 2 * W], q.INW[1]) + dot_nt(q.GM[s, :, 2 * W :], q.INW[2])
        put_part("R3", q.SB, q.OWNF, e, part)
        return carry

    lax.fori_loop(0, 4, product_back_step, 0)
    grad_out_in(1 - k)
    core_send("oi0")
    core_send("oi1")
    grad_out_in(k)

    grad_normed = reduce_sum("R3", q.SB, q.OWNF)

    def ffn_out_step(i, carry):
        e = far_first(i)
        s = mod(c + e, 4)
        put_part("RF", q.SBF, q.OWNF, e, dot(q.A[s], q.DNW[...]))
        return carry

    lax.fori_loop(0, 4, ffn_out_step, 0)
    stage_one("oi0")
    stage_one("oi1")

    def home(n):
        buf, out = ((q.MIXB, q.o_mixed), (q.GTB, q.o_gt))[n]
        base = 6 + 2 * n
        halves = lambda a: buf.at[:, pl.ds(pl.multiple_of(a * HALF, HALF), HALF)]
        rows = lambda j: out.at[pl.ds(j * T, T), :]
        near_local = pltpu.make_async_copy(halves(r), rows(k), q.sw_r.at[base])
        near_far = rcopy(halves(r), rows(k), q.sw_s.at[base], q.sw_r.at[base + 1], mate)
        away = rcopy(halves(1 - r), rows(k), q.sw_s.at[base + 1], q.sw_r.at[base + k], dev(r_=1 - r, k_=r))
        return halves, rows, base, near_local, near_far, away

    def home_start(n):
        halves, rows, base, near_local, near_far, away = home(n)

        @pl.when(same)
        def _():
            near_local.start()

        @pl.when(other)
        def _():
            near_far.start()

        away.start()

    def home_wait(n):
        halves, rows, base, near_local, near_far, away = home(n)

        @pl.when(same)
        def _():
            near_local.wait()
            rcopy(halves(r), rows(1 - k), q.sw_s.at[base], q.sw_r.at[base + 1], mate).wait_recv()

        @pl.when(other)
        def _():
            near_far.wait_send()
            for j in (0, 1):
                rcopy(halves(r), rows(j), q.sw_s.at[base], q.sw_r.at[base + j], dev(r_=1 - r)).wait_recv()

        away.wait_send()

    inputs = q.X[...].astype(F32)
    back, grad_gain = norm_back(inputs, norm_scale(inputs), q.GA[0:1, :], grad_normed)
    q.SM[0:1, :] = grad_gain
    q.GTB[...] = (q.OWN[...] + back).astype(BF)
    home_start(1)

    small_core = rcopy(q.SM, q.SMC, q.SM_s.at[0], q.SM_r.at[0], mate)
    small_core.start()
    for name in ("dn0", "dn1", "gt", "up"):
        stage_two(name)
    small_core.wait()

    def small_step(buf, me, base, target, value, rows):
        buf[me] = value
        for d in (1, 2, 3):
            rcopy(buf.at[me], buf.at[me], q.SM_s.at[base + d - 1], q.SM_r.at[base + d - 1], target(d)).start()

    def small_take(buf, me, base, target):
        for d in (1, 2, 3):
            rcopy(buf.at[me], buf.at[me], q.SM_s.at[base + d - 1], q.SM_r.at[base + d - 1], target(d)).wait_send()
            src = mod(me - d, 4)
            rcopy(buf.at[src], buf.at[src], q.SM_s.at[base + d - 1], q.SM_r.at[base + d - 1], target(d)).wait_recv()
        return (buf[0] + buf[1]) + (buf[2] + buf[3])

    small_step(q.SMX, x, 1, at_x, q.SM[...] + q.SMC[...], 8)
    for name in ("dn0", "dn1", "gt", "up"):
        stage_three(name)
    stage_two("oi0")
    stage_two("oi1")
    total = small_take(q.SMX, x, 1, at_x)
    small_step(q.SMY, y, 4, at_y, total, 8)
    q.MIXB[...] = (q.HID[...] + reduce_sum("RF", q.SBF, q.OWNF)).astype(BF)
    home_start(0)
    for name in ("dn0", "dn1", "gt", "up"):
        stage_four(name)
    stage_three("oi0")
    stage_three("oi1")
    total = small_take(q.SMY, y, 4, at_y)
    small_step(q.SMZ, c, 7, at_z, total, 8)
    stage_four("oi0")
    stage_four("oi1")
    for name in ("dn0", "dn1", "gt", "up"):
        stage_five(name)
    q.o_small[...] = total
    total = small_take(q.SMZ, c, 7, at_z)
    q.o_small[0:2, :] = total[0:2, :]
    stage_five("oi0")
    stage_five("oi1")
    home_wait(0)
    home_wait(1)
    gain_send.wait_send()
    for w in range(4):
        weight_end(w)
    for name in ("dn0", "dn1", "gt", "up", "oi0", "oi1"):
        stage_six(name)


def per_device(
    tokens,
    mixer_gain,
    in_weight,
    conv_kernel,
    out_weight,
    ffn_gain,
    gate_up_weight,
    down_weight,
    conv_reach,
    cotangent,
):
    reach = jnp.broadcast_to(conv_reach.astype(BF).reshape(2, 2, T, 1), (2, 2, T, 128))
    gains = jnp.concatenate([mixer_gain[None], ffn_gain[None], jnp.zeros((6, HALF), F32)], axis=0)
    hbm = pl.BlockSpec(memory_space=pl.ANY)
    vmem = pl.BlockSpec(memory_space=pltpu.VMEM)
    mixed, grad_tokens, small, g_in, g_out, g_gu, g_dn = pl.pallas_call(
        kernel,
        out_shape=(
            jax.ShapeDtypeStruct((2 * T, HALF), BF),
            jax.ShapeDtypeStruct((2 * T, HALF), BF),
            jax.ShapeDtypeStruct((8, D), F32),
            jax.ShapeDtypeStruct((3, 2, 2, 4, 32, W), BF),
            jax.ShapeDtypeStruct((2, 4, 32, HALF), BF),
            jax.ShapeDtypeStruct((2, 2, 2, 4, 32, H), BF),
            jax.ShapeDtypeStruct((2, 4, 144, HALF), BF),
        ),
        in_specs=[hbm, hbm, hbm, hbm, vmem, hbm, hbm, hbm, hbm],
        out_specs=(hbm, hbm, vmem, hbm, hbm, hbm, hbm),
        scratch_shapes=list(scratch_list().values()),
        compiler_params=pltpu.CompilerParams(
            collective_id=0, has_side_effects=True, vmem_limit_bytes=60 * 2**20
        ),
        name="block_step",
    )(tokens, cotangent, reach, gains, conv_kernel, in_weight, out_weight, gate_up_weight, down_weight)
    mine = lax.dynamic_slice_in_dim(small, lax.axis_index("row") * HALF, HALF, axis=1)
    return (
        mixed,
        grad_tokens.astype(F32),
        mine[0],
        g_in.reshape(3, HALF, W).astype(F32),
        small[2:5, :W],
        g_out.reshape(W, HALF).astype(F32),
        mine[1],
        g_gu.reshape(2, HALF, H).astype(F32),
        g_dn.reshape(H, HALF).astype(F32),
    )


def solution(mesh):
    return jax.shard_map(
        per_device,
        mesh=mesh,
        in_specs=(
            P(("dp", "col"), "row"),
            P("row"),
            P(None, "row", "col"),
            P(None, "col"),
            P("col", "row"),
            P("row"),
            P(None, "row", "col"),
            P("col", "row"),
            P(("dp", "row")),
            P(("dp", "col"), "row"),
        ),
        out_specs=(
            P(("dp", "col"), "row"),
            P(("dp", "col"), "row"),
            P("row"),
            P(None, "row", "col"),
            P(None, "col"),
            P("col", "row"),
            P("row"),
            P(None, "row", "col"),
            P("col", "row"),
        ),
        check_vma=False,
    )
```

```python
import functools

import jax
import jax.numpy as jnp
from jax import lax
from jax.experimental import pallas as pl
from jax.experimental.pallas import tpu as pltpu
from jax.sharding import PartitionSpec as P

MESH = pl.DeviceIdType.MESH
D = 1024
HALF = 512
T = 128
W = 256
H = 1152
EPS = 1e-05
F32 = jnp.float32
BF = jnp.bfloat16

UNITS = (("dn0", 144, 128, 0), ("dn1", 144, 128, 1), ("gt", 32, H, 0), ("up", 32, H, 1), ("oi0", 32, 512, 0), ("oi1", 32, 512, 1))


def mod(a, n):
    return lax.rem(a + 4 * n, n)


def dot(a, b):
    return lax.dot_general(a, b, (((1,), (0,)), ((), ())), preferred_element_type=F32)


def dot_nt(a, b):
    return lax.dot_general(a, b, (((1,), (1,)), ((), ())), preferred_element_type=F32)


def dot_tn(a, b):
    return lax.dot_general(a, b, (((0,), (0,)), ((), ())), preferred_element_type=F32)


def scratch_list():
    s = {}
    dma = pltpu.SemaphoreType.DMA

    def v(name, shape, dtype):
        s[name] = pltpu.VMEM(shape, dtype)

    v("INW", (3, D, W), BF)
    v("OUTF", (4, 4, 2, 32, D), BF)
    s["o_s"] = dma((8,))
    s["o_r"] = dma((8,))
    s["o_l"] = dma((1,))
    v("GUW", (2, D, H), BF)
    v("DNW", (H, D), BF)
    v("M", (4, T, 128), BF)
    v("GA", (8, D), F32)
    for n in ("XF", "COT", "GB", "GF"):
        v(n, (4, T, D) if n != "GF" else (4, 4 * T, W), BF)
        s[n + "_s"] = dma((6,))
        s[n + "_r"] = dma((6,))
    v("N1", (4, T, D), BF)
    v("N2", (4, T, D), BF)
    v("GGS", (4, T, W), BF)
    v("GGR", (4, T, W), BF)
    s["GG_s"] = dma((4,))
    s["GG_r"] = dma((4,))
    v("PR", (5, T + 8, W), F32)
    for n in ("GBV", "GCV", "VAL", "CO", "GCONV"):
        v(n, (4, T, W), F32)
    v("FM", (2, 5, T + 8, W), F32)
    v("HID", (T, D), F32)
    v("A", (4, T, H), BF)
    v("GG", (4, T, 2 * H), BF)
    v("GM", (4, T, 3 * W), BF)
    v("OWN", (T, D), F32)
    v("OWNF", (T, D), F32)
    for n in ("R2", "R3", "RF"):
        v(n, (2, T, D), BF)
        v(n + "_T", (2, T // 2, D), BF)
        v(n + "_B", (3, T, D), BF)
        s[n + "_s"] = dma((6,))
        s[n + "_r"] = dma((6,))
    v("MIXB", (T, D), BF)
    v("GTB", (T, D), BF)
    v("SM", (8, D), F32)
    v("SMC", (8, D), F32)
    v("SMX", (4, 8, D), F32)
    v("SMY", (4, 8, D), F32)
    v("SMZ", (4, 8, D), F32)
    s["SM_s"] = dma((12,))
    s["SM_r"] = dma((12,))
    s["sw_s"] = dma((10,))
    s["sw_r"] = dma((10,))
    s["ga"] = dma((3,))
    s["w_l"] = dma((4,))
    s["w_s"] = dma((12,))
    s["w_r"] = dma((12,))
    s["halo"] = dma((4,))
    for n, m, k, _ in UNITS:
        v(n + "_W", (2, 4, 4, m, k), BF)
        v(n + "_C", (4, 4, m, k), BF)
        v(n + "_R1", (3, 4, m, k), BF)
        v(n + "_S", (4, m, k), BF)
        v(n + "_R2", (3, m, k), BF)
        v(n + "_O", (2, 4, m, k), BF)
        s[n + "_s"] = dma((14,))
        s[n + "_r"] = dma((14,))
        s[n + "_l"] = dma((2,))
    return s


IN_NAMES = ("tok", "cot", "reach", "gains", "ck", "inw", "outw", "guw", "dnw")
OUT_NAMES = ("o_mixed", "o_gt", "o_small", "o_in", "o_out", "o_gu", "o_dn")


class Refs:
    pass


def kernel(*refs):
    q = Refs()
    names = IN_NAMES + OUT_NAMES + tuple(scratch_list())
    for name, ref in zip(names, refs, strict=True):
        setattr(q, name, ref)

    dp = lax.axis_index("dp")
    r = lax.axis_index("row")
    c = lax.axis_index("col")
    yhi = lax.div(dp, 8)
    x = lax.rem(lax.div(dp, 2), 4)
    k = lax.rem(dp, 2)
    y = yhi * 2 + r
    same = k == r
    other = k != r

    def dev(yhi_=None, x_=None, k_=None, r_=None, c_=None):
        yhi_ = yhi if yhi_ is None else yhi_
        x_ = x if x_ is None else x_
        k_ = k if k_ is None else k_
        return {"dp": yhi_ * 8 + x_ * 2 + k_, "row": r if r_ is None else r_, "col": c if c_ is None else c_}

    def at_y(d):
        to = mod(y + d, 4)
        return dev(yhi_=lax.div(to, 2), r_=lax.rem(to, 2))

    def at_x(d):
        return dev(x_=mod(x + d, 4))

    def at_z(d):
        return dev(c_=mod(c + d, 4))

    mate = dev(k_=1 - k)

    def slot_y(d):
        to = mod(y + d, 4)
        return lax.rem(to, 2) * 2 + lax.div(to, 2)

    def rcopy(src, dst, ss, rs, to):
        return pltpu.make_async_remote_copy(
            src_ref=src, dst_ref=dst, send_sem=ss, recv_sem=rs, device_id=to, device_id_type=MESH
        )

    barrier = pltpu.get_barrier_semaphore()
    friends = [mate, dev(r_=1 - r, k_=1 - k)]
    friends += [f(d) for f in (at_x, at_y, at_z) for d in (1, 2, 3)]
    for to in friends:
        pl.semaphore_signal(barrier, inc=1, device_id=to, device_id_type=MESH)
    pl.semaphore_wait(barrier, len(friends))

    def weight_regions(w):
        if w == 0:
            return (q.inw, q.INW, lambda p, n, a: (q.inw.at[:, pl.ds(p * 128, 128 * n), :], q.INW.at[:, pl.ds(a * HALF + p * 128, 128 * n), :]))
        if w == 2:
            return (q.guw, q.GUW, lambda p, n, a: (q.guw.at[:, pl.ds(p * 128, 128 * n), :], q.GUW.at[:, pl.ds(a * HALF + p * 128, 128 * n), :]))
        return (q.dnw, q.DNW, lambda p, n, a: (q.dnw.at[pl.ds(p * 288, 288 * n), :], q.DNW.at[pl.ds(p * 288, 288 * n), pl.ds(pl.multiple_of(a * HALF, HALF), HALF)]))

    def weight_local(w):
        _, _, region = weight_regions(w)
        src, dst = region(0, 4, r)
        return pltpu.make_async_copy(src, dst, q.w_l.at[w])

    def weight_send(w, s):
        _, _, region = weight_regions(w)
        src, dst = region(k * 2 + s, 1, r)
        return rcopy(src, dst, q.w_s.at[w * 3 + s], q.w_r.at[w * 3 + s], at_y(1 - 2 * s))

    def weight_arrival(w, s):
        _, _, region = weight_regions(w)
        src, _ = region(k * 2 + s, 1, r)
        _, dst = region(k * 2 + s, 1, 1 - r)
        return rcopy(src, dst, q.w_s.at[w * 3 + s], q.w_r.at[w * 3 + s], at_y(1 - 2 * s))

    def weight_pass(w, core):
        _, _, region = weight_regions(w)
        _, dst = region(core * 2, 2, 1 - r)
        return rcopy(dst, dst, q.w_s.at[w * 3 + 2], q.w_r.at[w * 3 + 2], mate)

    def weight_start(w):
        for s in (0, 1):
            weight_send(w, s).start()

    def weight_forward(w):
        for s in (0, 1):
            weight_arrival(w, s).wait_recv()
        weight_pass(w, k).start()

    def weight_ready(w):
        weight_local(w).wait()
        weight_pass(w, 1 - k).wait_recv()

    def weight_end(w):
        for s in (0, 1):
            weight_send(w, s).wait_send()
        weight_pass(w, k).wait_send()

    for w in (0, 2, 3):
        weight_local(w).start()

    half = lambda a: pl.ds(pl.multiple_of(a * HALF, HALF), HALF)
    out_own = q.outw.at[pl.ds(x * 64 + k * 32, 32), :]
    out_local = pltpu.make_async_copy(out_own, q.OUTF.at[c, x, k, :, half(r)], q.o_l.at[0])

    def out_row(a):
        return rcopy(out_own, q.OUTF.at[c, x, k, :, half(a)], q.o_s.at[0], q.o_r.at[0], dev(r_=1 - r))

    def out_col(d, a):
        view = q.OUTF.at[a, x, k]
        return rcopy(view, view, q.o_s.at[d], q.o_r.at[d], at_z(d))

    def out_x(d, a):
        view = q.OUTF.at[:, a, k]
        return rcopy(view, view, q.o_s.at[3 + d], q.o_r.at[3 + d], at_x(d))

    def out_core(core):
        view = q.OUTF.at[:, :, core]
        return rcopy(view, view, q.o_s.at[7], q.o_r.at[7], mate)

    def out_stage_col():
        out_local.wait()
        out_row(1 - r).wait_recv()
        for d in (1, 3, 2):
            out_col(d, c).start()

    def out_stage_x():
        for d in (1, 3, 2):
            out_col(d, mod(c - d, 4)).wait_recv()
        for d in (1, 3, 2):
            out_x(d, x).start()

    def out_stage_core():
        for d in (1, 3, 2):
            out_x(d, mod(x - d, 4)).wait_recv()
        out_core(k).start()

    def out_ready():
        out_core(1 - k).wait_recv()
        out_row(r).wait_send()
        for d in (1, 2, 3):
            out_col(d, c).wait_send()
            out_x(d, x).wait_send()
        out_core(k).wait_send()

    def swap_views(n):
        if n == 0:
            return lambda j: q.tok.at[pl.ds(j * T, T), :], lambda a: q.XF.at[c, :, pl.ds(pl.multiple_of(a * HALF, HALF), HALF)]
        if n == 1:
            return lambda j: q.reach.at[:, j], lambda a: q.M.at[pl.ds(2 * a, 2)]
        return lambda j: q.cot.at[pl.ds(j * T, T), :], lambda a: q.COT.at[c, :, pl.ds(pl.multiple_of(a * HALF, HALF), HALF)]

    def swap_near(n):
        src, dst = swap_views(n)
        return (
            pltpu.make_async_copy(src(k), dst(r), q.sw_r.at[2 * n]),
            rcopy(src(1 - k), dst(r), q.sw_s.at[2 * n], q.sw_r.at[2 * n], mate),
        )

    def swap_far(n, j):
        src, dst = swap_views(n)
        return rcopy(src(j), dst(r), q.sw_s.at[2 * n + j], q.sw_r.at[2 * n + 1], dev(r_=1 - r, k_=j))

    def swap_start(n):
        @pl.when(same)
        def _():
            near, far = swap_near(n)
            near.start()
            far.start()

        @pl.when(other)
        def _():
            swap_far(n, 0).start()
            swap_far(n, 1).start()

    def swap_wait(n):
        src, dst = swap_views(n)

        @pl.when(same)
        def _():
            near, far = swap_near(n)
            near.wait()
            far.wait_send()

        @pl.when(other)
        def _():
            swap_far(n, 0).wait_send()
            swap_far(n, 1).wait_send()
            rcopy(src(1 - k), dst(r), q.sw_s.at[2 * n], q.sw_r.at[2 * n], mate).wait_recv()

        rcopy(src(0), dst(1 - r), q.sw_s.at[2 * n], q.sw_r.at[2 * n + 1], dev(r_=1 - r)).wait_recv()

    def gain_view(a):
        return q.GA.at[:, pl.ds(pl.multiple_of(a * HALF, HALF), HALF)]

    gain_local = pltpu.make_async_copy(q.gains, gain_view(r), q.ga.at[0])
    gain_send = rcopy(q.gains, gain_view(r), q.ga.at[1], q.ga.at[2], dev(r_=1 - r))
    gain_take = rcopy(q.gains, gain_view(1 - r), q.ga.at[1], q.ga.at[2], dev(r_=1 - r))

    swap_start(0)
    gain_local.start()
    gain_send.start()
    out_local.start()
    out_row(r).start()
    weight_start(0)
    swap_start(1)

    def gather(name, n, a):
        buf = getattr(q, name)
        rows = buf.shape[1] // 2
        h = (0, 1, 1, 0, 0, 1)[n]
        view = buf.at[a, pl.ds(h * rows, rows)]
        return rcopy(view, view, getattr(q, name + "_s").at[n], getattr(q, name + "_r").at[n], at_z(3 if n in (1, 3, 5) else 1))

    def gather_start(name, parts=(0, 1, 2, 3)):
        for n in parts:
            gather(name, n, c).start()

    def gather_pass(name):
        gather(name, 0, mod(c - 1, 4)).wait_recv()
        gather(name, 4, mod(c - 1, 4)).start()
        gather(name, 1, mod(c + 1, 4)).wait_recv()
        gather(name, 5, mod(c + 1, 4)).start()

    def gather_take(name, d):
        if d == 1:
            gather(name, 2, mod(c - 1, 4)).wait_recv()
        elif d == 3:
            gather(name, 3, mod(c + 1, 4)).wait_recv()
        else:
            gather(name, 4, mod(c + 2, 4)).wait_recv()
            gather(name, 5, mod(c + 2, 4)).wait_recv()

    def gather_step(name, i):
        for n, d in ((1, 1), (2, 3), (3, 2)):

            @pl.when(i == n)
            def _():
                if n == 1:
                    gather_pass(name)
                gather_take(name, d)

    def gather_end(name):
        for n in (0, 1, 2, 3):
            gather(name, n, c).wait_send()
        gather(name, 4, mod(c - 1, 4)).wait_send()
        gather(name, 5, mod(c + 1, 4)).wait_send()

    HT = T // 2

    def reduce_copy(name, n):
        buf, mid, send = getattr(q, name), getattr(q, name + "_T"), getattr(q, name + "_B")
        src, dst, d = (
            (send.at[1, 0:HT], mid.at[0], 1),
            (send.at[1, HT:T], mid.at[1], 3),
            (send.at[0, HT:T], buf.at[0, HT:T], 1),
            (send.at[0, 0:HT], buf.at[0, 0:HT], 1),
            (send.at[2, 0:HT], buf.at[1, 0:HT], 3),
            (send.at[2, HT:T], buf.at[1, HT:T], 3),
        )[n]
        return rcopy(src, dst, getattr(q, name + "_s").at[n], getattr(q, name + "_r").at[n], at_z(d))

    def reduce_sum(name, own):
        buf = getattr(q, name)
        for n in (2, 4, 3, 5):
            reduce_copy(name, n).wait_recv()
        for n in range(6):
            reduce_copy(name, n).wait_send()
        return own[...] + (buf[0].astype(F32) + buf[1].astype(F32))

    def put_part(name, own, e, part):
        mid, send = getattr(q, name + "_T"), getattr(q, name + "_B")

        @pl.when(e == 0)
        def _():
            own[...] = part

        @pl.when(e == 2)
        def _():
            send[1] = part.astype(BF)
            reduce_copy(name, 0).start()
            reduce_copy(name, 1).start()

        @pl.when(e == 1)
        def _():
            send[0, HT:T] = part[HT:].astype(BF)
            reduce_copy(name, 2).start()
            reduce_copy(name, 0).wait_recv()
            send[0, 0:HT] = (part[:HT] + mid[0].astype(F32)).astype(BF)
            reduce_copy(name, 3).start()

        @pl.when(e == 3)
        def _():
            send[2, 0:HT] = part[:HT].astype(BF)
            reduce_copy(name, 4).start()
            reduce_copy(name, 1).wait_recv()
            send[2, HT:T] = (part[HT:] + mid[1].astype(F32)).astype(BF)
            reduce_copy(name, 5).start()

    def arrival(i):
        return i + lax.div(i, 2) - 2 * lax.div(i, 3)

    def far_first(i):
        return mod(2 - i + 3 * lax.div(i, 2) - 2 * lax.div(i, 3), 4)

    def norm_scale(value):
        return lax.rsqrt(jnp.sum(value * value, axis=1, keepdims=True) / D + EPS)

    swap_wait(0)
    gather_start("XF")
    swap_start(2)
    for w in (2, 3):
        weight_start(w)
    out_stage_col()
    gain_local.wait()
    gain_take.wait_recv()
    weight_forward(0)
    weight_ready(0)

    @pl.when(k == 0)
    def _():
        q.PR[0, 0:8] = jnp.zeros((8, W), F32)

    def in_step(i, carry):
        s = mod(c - arrival(i), 4)
        gather_step("XF", i)
        inputs = q.XF[s].astype(F32)
        q.N1[s] = (inputs * norm_scale(inputs) * q.GA[0:1, :]).astype(BF)
        rows = q.N1[s]
        b = dot(rows, q.INW[0])
        v = dot(rows, q.INW[2])
        q.GBV[s] = b
        q.VAL[s] = v
        q.PR[s, 8:] = b * v
        q.GCV[s] = dot(rows, q.INW[1])
        return carry

    lax.fori_loop(0, 4, in_step, 0)
    halo_f = rcopy(q.PR.at[0:4, pl.ds(T, 8)], q.PR.at[pl.ds(k, 4), 0:8], q.halo.at[0], q.halo.at[1], mate)
    halo_ft = rcopy(q.PR.at[0:4, pl.ds(T, 8)], q.PR.at[pl.ds(1 - k, 4), 0:8], q.halo.at[0], q.halo.at[1], mate)
    halo_f.start()
    gather_end("XF")
    out_stage_x()
    swap_wait(2)
    swap_wait(1)
    halo_f.wait_send()
    halo_ft.wait_recv()

    def masks(s):
        reach = q.M[s].astype(F32)
        first = jnp.where(reach >= 1.0, 1.0, 0.0)
        second = jnp.where(reach >= 2.0, 1.0, 0.0)
        return jnp.concatenate([first, first], axis=1), jnp.concatenate([second, second], axis=1)

    def conv_step(s, carry):
        m1, m2 = masks(s)
        conv = q.ck[0:1, :] * q.PR[s, pl.ds(8, T)]
        conv = conv + q.ck[1:2, :] * q.PR[s, pl.ds(7, T)] * m1
        conv = conv + q.ck[2:3, :] * q.PR[s, pl.ds(6, T)] * m2
        q.CO[s] = conv
        q.GF[c, pl.ds(pl.multiple_of(s * T, T), T)] = (q.GCV[s] * conv).astype(BF)
        return carry

    lax.fori_loop(0, 2, conv_step, 0)
    gather_start("GF", (0, 3))
    lax.fori_loop(2, 4, conv_step, 0)
    gather_start("GF", (1, 2))
    gather_start("COT")
    weight_forward(2)
    out_stage_core()
    gather_pass("GF")
    weight_forward(3)
    for d in (1, 3, 2):
        gather_take("GF", d)
    gather_pass("COT")
    out_ready()
    weight_ready(2)
    weight_ready(3)
    for d in (1, 3, 2):
        gather_take("COT", d)

    def ffn_step(i, carry):
        e = far_first(i)
        s = mod(c + e, 4)
        at = pl.ds(pl.multiple_of(s * T, T), T)
        gated = jnp.concatenate([q.GF[n, at] for n in range(4)], axis=1)
        hidden = q.XF[s].astype(F32) + dot(gated, q.OUTF[...].reshape(D, D))

        @pl.when(e == 0)
        def _():
            q.HID[...] = hidden

        q.N2[s] = (hidden * norm_scale(hidden) * q.GA[1:2, :]).astype(BF)
        rows = q.N2[s]
        gate = dot(rows, q.GUW[0])
        up = dot(rows, q.GUW[1])
        sig = 1.0 / (1.0 + jnp.exp(-gate))
        silu = gate * sig
        q.A[s] = (silu * up).astype(BF)
        ga = dot_nt(q.COT[s], q.DNW[...])
        q.GG[s, :, 0:H] = (ga * up * sig * (1.0 + gate * (1.0 - sig))).astype(BF)
        q.GG[s, :, H:] = (ga * silu).astype(BF)
        part = dot_nt(q.GG[s, :, 0:H], q.GUW[0]) + dot_nt(q.GG[s, :, H:], q.GUW[1])
        put_part("R2", q.OWN, e, part)
        return carry

    lax.fori_loop(0, 4, ffn_step, 0)
    gather_end("GF")
    gather_end("COT")

    def unit(name):
        return next(u for u in UNITS if u[0] == name)

    def g(name, what):
        return getattr(q, name + "_" + what)

    def core_copy(name, core):
        return rcopy(g(name, "W").at[core], g(name, "C"), g(name, "s").at[0], g(name, "r").at[0], mate)

    def first_copy(name, d):
        w = g(name, "W")
        if unit(name)[3] == 0:
            src, to = w.at[k, :, mod(x + d, 4)], at_x(d)
        else:
            src, to = w.at[k, slot_y(d)], at_y(d)
        return rcopy(src, g(name, "R1").at[d - 1], g(name, "s").at[d], g(name, "r").at[d], to)

    def second_copy(name, d):
        if unit(name)[3] == 0:
            src, to = g(name, "S").at[slot_y(d)], at_y(d)
        else:
            src, to = g(name, "S").at[mod(x + d, 4)], at_x(d)
        return rcopy(src, g(name, "R2").at[d - 1], g(name, "s").at[3 + d], g(name, "r").at[3 + d], to)

    def spread_x(name, d, place):
        o = g(name, "O")
        view = o.at[:, place] if unit(name)[3] == 0 else o.at[yhi, place]
        return rcopy(view, view, g(name, "s").at[6 + d], g(name, "r").at[6 + d], at_x(d))

    def spread_y(name, place):
        o = g(name, "O")
        view = o.at[place, x] if unit(name)[3] == 0 else o.at[place]
        return rcopy(view, view, g(name, "s").at[10], g(name, "r").at[10], at_y(2))

    def core_send(name):
        core_copy(name, 1 - k).start()

    def stage_one(name):
        core_copy(name, 1 - k).wait()
        w, other_part = g(name, "W"), g(name, "C")

        def add(i, carry):
            a, b = lax.div(i, 4), lax.rem(i, 4)
            w[k, a, b] = (w[k, a, b].astype(F32) + other_part[a, b].astype(F32)).astype(BF)
            return carry

        lax.fori_loop(0, 16, add, 0)
        for d in (1, 3, 2):
            first_copy(name, d).start()

    def stage_two(name):
        for d in (1, 3, 2):
            first_copy(name, d).wait()
        w, got, total = g(name, "W"), g(name, "R1"), g(name, "S")

        def add(i, carry):
            mine = w[k, i, x] if unit(name)[3] == 0 else w[k, slot_y(0), i]
            total[i] = (mine.astype(F32) + got[0, i].astype(F32) + got[1, i].astype(F32) + got[2, i].astype(F32)).astype(BF)
            return carry

        lax.fori_loop(0, 4, add, 0)
        for d in (1, 3, 2):
            second_copy(name, d).start()

    def stage_three(name):
        for d in (1, 3, 2):
            second_copy(name, d).wait()
        got, total = g(name, "R2"), g(name, "S")
        mine = total[slot_y(0)] if unit(name)[3] == 0 else total[x]
        g(name, "O")[yhi, x] = (mine.astype(F32) + got[0].astype(F32) + got[1].astype(F32) + got[2].astype(F32)).astype(BF)
        if unit(name)[3] == 0:
            spread_y(name, yhi).start()
        else:
            for d in (1, 3, 2):
                spread_x(name, d, x).start()

    def take_x(name):
        for d in (1, 3, 2):
            spread_x(name, d, x).wait_send()
            spread_x(name, d, mod(x - d, 4)).wait_recv()

    def take_y(name):
        spread_y(name, yhi).wait_send()
        spread_y(name, 1 - yhi).wait_recv()

    def stage_four(name):
        if unit(name)[3] == 0:
            take_y(name)
            for d in (1, 3, 2):
                spread_x(name, d, x).start()
        else:
            take_x(name)
            spread_y(name, yhi).start()

    def results(name, core):
        o = g(name, "O")
        half = unit(name)[3]
        if name in ("dn0", "dn1"):
            at = pl.multiple_of(core * W + half * 128, 128)
            return [(o, q.o_dn.at[:, :, :, pl.ds(at, 128)])]
        if name in ("gt", "up"):
            return [(o, q.o_gu.at[half, core])]
        if name == "oi0":
            at = pl.multiple_of(core * W, W)
            return [(o.at[:, :, :, 0:W], q.o_out.at[:, :, :, pl.ds(at, W)]), (o.at[:, :, :, W:], q.o_in.at[0, core])]
        return [(o.at[:, :, :, 0:W], q.o_in.at[1, core]), (o.at[:, :, :, W:], q.o_in.at[2, core])]

    def stage_five(name):
        if unit(name)[3] == 0:
            take_x(name)
        else:
            take_y(name)
        for n, (src, dst) in enumerate(results(name, k)):
            pltpu.make_async_copy(src, dst, g(name, "l").at[n]).start()
            rcopy(src, dst, g(name, "s").at[11 + n], g(name, "r").at[11 + n], mate).start()

    def stage_six(name):
        for n, (src, dst) in enumerate(results(name, k)):
            pltpu.make_async_copy(src, dst, g(name, "l").at[n]).wait()
            rcopy(src, dst, g(name, "s").at[11 + n], g(name, "r").at[11 + n], mate).wait_send()
        for n, (src, dst) in enumerate(results(name, 1 - k)):
            rcopy(src, dst, g(name, "s").at[11 + n], g(name, "r").at[11 + n], mate).wait_recv()

    def features(ref, a, core):
        at = pl.multiple_of(a * HALF + core * W, W)
        return ref[:, :, pl.ds(at, W)].reshape(4 * T, W)

    def grad_down(core):
        def step(a, carry):
            full = dot_tn(q.A[...].reshape(4 * T, H), features(q.COT, a, core)).astype(BF).reshape(2, 4, 144, W)
            q.dn0_W[core, pl.ds(2 * a, 2)] = full[:, :, :, :128]
            q.dn1_W[core, pl.ds(2 * a, 2)] = full[:, :, :, 128:]
            return carry

        lax.fori_loop(0, 2, step, 0)

    def grad_gate_up(core):
        def step(a, carry):
            rows = features(q.N2, a, core)
            q.gt_W[core, pl.ds(2 * a, 2)] = dot_tn(rows, q.GG[:, :, 0:H].reshape(4 * T, H)).astype(BF).reshape(2, 4, 32, H)
            q.up_W[core, pl.ds(2 * a, 2)] = dot_tn(rows, q.GG[:, :, H:].reshape(4 * T, H)).astype(BF).reshape(2, 4, 32, H)
            return carry

        lax.fori_loop(0, 2, step, 0)

    def grad_out_in(core):
        def step(a, carry):
            rows = features(q.N1, a, core)
            gated = q.GF[c]
            q.oi0_W[core, pl.ds(2 * a, 2), :, :, 0:W] = dot_tn(gated, features(q.GB, a, core)).astype(BF).reshape(2, 4, 32, W)
            into = dot_tn(rows, q.GM[...].reshape(4 * T, 3 * W)).astype(BF).reshape(2, 4, 32, 3 * W)
            q.oi0_W[core, pl.ds(2 * a, 2), :, :, W:] = into[:, :, :, 0:W]
            q.oi1_W[core, pl.ds(2 * a, 2)] = into[:, :, :, W:]
            return carry

        lax.fori_loop(0, 2, step, 0)

    def norm_back(value, scale, gain, grad):
        weighted = grad * gain
        inner = jnp.sum(weighted * value, axis=1, keepdims=True)
        back = scale * weighted - value * (scale * scale * scale) * inner / D
        return back, jnp.sum(grad * value * scale, axis=0, keepdims=True)

    grad_down(1 - k)
    core_send("dn0")
    core_send("dn1")
    grad_gate_up(1 - k)
    core_send("gt")
    core_send("up")
    grad_down(k)
    stage_one("dn0")
    stage_one("dn1")
    grad_normed = reduce_sum("R2", q.OWN)
    hidden = q.HID[...]
    back, grad_gain = norm_back(hidden, norm_scale(hidden), q.GA[1:2, :], grad_normed)
    q.SM[...] = jnp.zeros((8, D), F32)
    q.SM[1:2, :] = grad_gain
    grad_hidden = q.COT[c].astype(F32) + back
    q.GB[c] = grad_hidden.astype(BF)
    q.OWN[...] = grad_hidden
    grad_gated = dot_nt(q.GB[c], q.OUTF[...].reshape(D, D)).astype(BF)
    for n in range(4):
        q.GGS[n] = grad_gated[:, n * W : (n + 1) * W]

    def gated_copy(d, dst):
        return rcopy(q.GGS.at[mod(c + d, 4)], q.GGR.at[dst], q.GG_s.at[d], q.GG_r.at[d], at_z(d))

    for d in (1, 3, 2):
        gated_copy(d, c).start()
    gather_start("GB")
    q.GGR[c] = q.GGS[c]
    grad_gate_up(k)
    stage_one("gt")
    stage_one("up")

    @pl.when(k == 1)
    def _():
        q.FM[0, 4, pl.ds(T, 8)] = jnp.zeros((8, W), F32)
        q.FM[1, 4, pl.ds(T, 8)] = jnp.zeros((8, W), F32)

    for d in (1, 3, 2):
        gated_copy(d, c).wait_send()
        gated_copy(d, mod(c - d, 4)).wait_recv()

    def conv_back_step(s, carry):
        grad_gated = q.GGR[s].astype(F32)
        q.GM[s, :, W : 2 * W] = (grad_gated * q.CO[s]).astype(BF)
        grad_conv = grad_gated * q.GCV[s]
        q.GCONV[s] = grad_conv
        m1, m2 = masks(s)
        q.FM[0, s + 1, 0:T] = grad_conv * m1
        q.FM[1, s + 1, 0:T] = grad_conv * m2
        return carry

    lax.fori_loop(0, 4, conv_back_step, 0)
    halo_b = rcopy(q.FM.at[:, 1:5, 0:8], q.FM.at[:, pl.ds(k, 4), pl.ds(T, 8)], q.halo.at[2], q.halo.at[3], mate)
    halo_bt = rcopy(q.FM.at[:, 1:5, 0:8], q.FM.at[:, pl.ds(1 - k, 4), pl.ds(T, 8)], q.halo.at[2], q.halo.at[3], mate)
    halo_b.start()
    gather_pass("GB")
    halo_b.wait_send()
    halo_bt.wait_recv()

    def product_back_step(i, carry):
        e = far_first(i)
        s = mod(c + e, 4)
        grad_conv = q.GCONV[s]
        grad_product = q.ck[0:1, :] * grad_conv
        grad_product = grad_product + q.ck[1:2, :] * q.FM[0, s + 1, pl.ds(1, T)]
        grad_product = grad_product + q.ck[2:3, :] * q.FM[1, s + 1, pl.ds(2, T)]
        q.SM[2:3, 0:W] += jnp.sum(grad_conv * q.PR[s, pl.ds(8, T)], axis=0, keepdims=True)
        q.SM[3:4, 0:W] += jnp.sum(q.FM[0, s + 1, pl.ds(0, T)] * q.PR[s, pl.ds(7, T)], axis=0, keepdims=True)
        q.SM[4:5, 0:W] += jnp.sum(q.FM[1, s + 1, pl.ds(0, T)] * q.PR[s, pl.ds(6, T)], axis=0, keepdims=True)
        q.GM[s, :, 0:W] = (grad_product * q.VAL[s]).astype(BF)
        q.GM[s, :, 2 * W :] = (grad_product * q.GBV[s]).astype(BF)
        part = dot_nt(q.GM[s, :, 0:W], q.INW[0]) + dot_nt(q.GM[s, :, W : 2 * W], q.INW[1]) + dot_nt(q.GM[s, :, 2 * W :], q.INW[2])
        put_part("R3", q.OWNF, e, part)
        return carry

    lax.fori_loop(0, 4, product_back_step, 0)
    for d in (1, 3, 2):
        gather_take("GB", d)
    grad_out_in(1 - k)
    core_send("oi0")
    core_send("oi1")
    grad_out_in(k)
    gather_end("GB")
    stage_two("dn0")
    stage_two("dn1")
    stage_one("oi0")
    stage_one("oi1")

    grad_normed = reduce_sum("R3", q.OWNF)

    def ffn_out_step(i, carry):
        e = far_first(i)
        s = mod(c + e, 4)
        put_part("RF", q.OWNF, e, dot(q.A[s], q.DNW[...]))
        return carry

    def home(n):
        buf, out = ((q.MIXB, q.o_mixed), (q.GTB, q.o_gt))[n]
        base = 6 + 2 * n
        halves = lambda a: buf.at[:, pl.ds(pl.multiple_of(a * HALF, HALF), HALF)]
        rows = lambda j: out.at[pl.ds(j * T, T), :]
        near_local = pltpu.make_async_copy(halves(r), rows(k), q.sw_r.at[base])
        near_far = rcopy(halves(r), rows(k), q.sw_s.at[base], q.sw_r.at[base + 1], mate)
        away = rcopy(halves(1 - r), rows(k), q.sw_s.at[base + 1], q.sw_r.at[base + k], dev(r_=1 - r, k_=r))
        return halves, rows, base, near_local, near_far, away

    def home_start(n):
        halves, rows, base, near_local, near_far, away = home(n)

        @pl.when(same)
        def _():
            near_local.start()

        @pl.when(other)
        def _():
            near_far.start()

        away.start()

    def home_wait(n):
        halves, rows, base, near_local, near_far, away = home(n)

        @pl.when(same)
        def _():
            near_local.wait()
            rcopy(halves(r), rows(1 - k), q.sw_s.at[base], q.sw_r.at[base + 1], mate).wait_recv()

        @pl.when(other)
        def _():
            near_far.wait_send()
            for j in (0, 1):
                rcopy(halves(r), rows(j), q.sw_s.at[base], q.sw_r.at[base + j], dev(r_=1 - r)).wait_recv()

        away.wait_send()

    inputs = q.XF[c].astype(F32)
    back, grad_gain = norm_back(inputs, norm_scale(inputs), q.GA[0:1, :], grad_normed)
    q.SM[0:1, :] = grad_gain
    q.GTB[...] = (q.OWN[...] + back).astype(BF)
    home_start(1)

    small_core = rcopy(q.SM, q.SMC, q.SM_s.at[0], q.SM_r.at[0], mate)
    small_core.start()
    lax.fori_loop(0, 4, ffn_out_step, 0)
    stage_two("gt")
    stage_two("up")
    stage_three("dn0")
    stage_three("dn1")
    small_core.wait()

    def small_step(buf, me, base, target, value, rows):
        buf[me] = value
        for d in (1, 2, 3):
            rcopy(buf.at[me], buf.at[me], q.SM_s.at[base + d - 1], q.SM_r.at[base + d - 1], target(d)).start()

    def small_take(buf, me, base, target):
        for d in (1, 2, 3):
            rcopy(buf.at[me], buf.at[me], q.SM_s.at[base + d - 1], q.SM_r.at[base + d - 1], target(d)).wait_send()
            src = mod(me - d, 4)
            rcopy(buf.at[src], buf.at[src], q.SM_s.at[base + d - 1], q.SM_r.at[base + d - 1], target(d)).wait_recv()
        return (buf[0] + buf[1]) + (buf[2] + buf[3])

    small_step(q.SMX, x, 1, at_x, q.SM[...] + q.SMC[...], 8)
    stage_two("oi0")
    stage_two("oi1")
    stage_three("gt")
    stage_three("up")
    stage_four("dn0")
    stage_four("dn1")
    total = small_take(q.SMX, x, 1, at_x)
    small_step(q.SMY, y, 4, at_y, total, 8)
    q.MIXB[...] = (q.HID[...] + reduce_sum("RF", q.OWNF)).astype(BF)
    home_start(0)
    stage_four("gt")
    stage_four("up")
    stage_three("oi0")
    stage_three("oi1")
    total = small_take(q.SMY, y, 4, at_y)
    small_step(q.SMZ, c, 7, at_z, total, 8)
    stage_five("dn0")
    stage_five("dn1")
    stage_four("oi0")
    stage_four("oi1")
    stage_five("gt")
    stage_five("up")
    q.o_small[...] = total
    total = small_take(q.SMZ, c, 7, at_z)
    q.o_small[0:2, :] = total[0:2, :]
    stage_five("oi0")
    stage_five("oi1")
    home_wait(0)
    home_wait(1)
    gain_send.wait_send()
    for w in (0, 2, 3):
        weight_end(w)
    for name in ("dn0", "dn1", "gt", "up", "oi0", "oi1"):
        stage_six(name)


def per_device(
    tokens,
    mixer_gain,
    in_weight,
    conv_kernel,
    out_weight,
    ffn_gain,
    gate_up_weight,
    down_weight,
    conv_reach,
    cotangent,
):
    reach = jnp.broadcast_to(conv_reach.astype(BF).reshape(2, 2, T, 1), (2, 2, T, 128))
    gains = jnp.concatenate([mixer_gain[None], ffn_gain[None], jnp.zeros((6, HALF), F32)], axis=0)
    hbm = pl.BlockSpec(memory_space=pl.ANY)
    vmem = pl.BlockSpec(memory_space=pltpu.VMEM)
    mixed, grad_tokens, small, g_in, g_out, g_gu, g_dn = pl.pallas_call(
        kernel,
        out_shape=(
            jax.ShapeDtypeStruct((2 * T, HALF), BF),
            jax.ShapeDtypeStruct((2 * T, HALF), BF),
            jax.ShapeDtypeStruct((8, D), F32),
            jax.ShapeDtypeStruct((3, 2, 2, 4, 32, W), BF),
            jax.ShapeDtypeStruct((2, 4, 32, HALF), BF),
            jax.ShapeDtypeStruct((2, 2, 2, 4, 32, H), BF),
            jax.ShapeDtypeStruct((2, 4, 144, HALF), BF),
        ),
        in_specs=[hbm, hbm, hbm, hbm, vmem, hbm, hbm, hbm, hbm],
        out_specs=(hbm, hbm, vmem, hbm, hbm, hbm, hbm),
        scratch_shapes=list(scratch_list().values()),
        compiler_params=pltpu.CompilerParams(
            collective_id=0, has_side_effects=True, vmem_limit_bytes=60 * 2**20
        ),
        name="block_step",
    )(tokens, cotangent, reach, gains, conv_kernel, in_weight, out_weight, gate_up_weight, down_weight)
    mine = lax.dynamic_slice_in_dim(small, lax.axis_index("row") * HALF, HALF, axis=1)
    return (
        mixed,
        grad_tokens.astype(F32),
        mine[0],
        g_in.reshape(3, HALF, W).astype(F32),
        small[2:5, :W],
        g_out.reshape(W, HALF).astype(F32),
        mine[1],
        g_gu.reshape(2, HALF, H).astype(F32),
        g_dn.reshape(H, HALF).astype(F32),
    )


def solution(mesh):
    return jax.shard_map(
        per_device,
        mesh=mesh,
        in_specs=(
            P(("dp", "col"), "row"),
            P("row"),
            P(None, "row", "col"),
            P(None, "col"),
            P("col", "row"),
            P("row"),
            P(None, "row", "col"),
            P("col", "row"),
            P(("dp", "row")),
            P(("dp", "col"), "row"),
        ),
        out_specs=(
            P(("dp", "col"), "row"),
            P(("dp", "col"), "row"),
            P("row"),
            P(None, "row", "col"),
            P(None, "col"),
            P("col", "row"),
            P("row"),
            P(None, "row", "col"),
            P("col", "row"),
        ),
        check_vma=False,
    )
```

```python
import functools

import jax
import jax.numpy as jnp
from jax import lax
from jax.experimental import pallas as pl
from jax.experimental.pallas import tpu as pltpu
from jax.sharding import PartitionSpec as P

MESH = pl.DeviceIdType.MESH
D = 1024
HALF = 512
T = 128
W = 256
H = 1152
EPS = 1e-05
F32 = jnp.float32
BF = jnp.bfloat16

UNITS = (("dn0", 144, 128, 0), ("dn1", 144, 128, 1), ("gt", 32, H, 0), ("up", 32, H, 1), ("oi0", 32, 512, 0), ("oi1", 32, 512, 1))


def mod(a, n):
    return lax.rem(a + 4 * n, n)


def dot(a, b):
    return lax.dot_general(a, b, (((1,), (0,)), ((), ())), preferred_element_type=F32)


def dot_nt(a, b):
    return lax.dot_general(a, b, (((1,), (1,)), ((), ())), preferred_element_type=F32)


def dot_tn(a, b):
    return lax.dot_general(a, b, (((0,), (0,)), ((), ())), preferred_element_type=F32)


def scratch_list():
    s = {}
    dma = pltpu.SemaphoreType.DMA

    def v(name, shape, dtype):
        s[name] = pltpu.VMEM(shape, dtype)

    v("INW", (3, D, W), BF)
    v("OUTF", (4, 4, 2, 32, D), BF)
    s["o_s"] = dma((8,))
    s["o_r"] = dma((8,))
    s["o_l"] = dma((1,))
    v("GUW", (2, 2, 4, 2, 64, H), BF)
    s["gu_s"] = dma((3,))
    s["gu_r"] = dma((3,))
    for n in ("GUX", "OUX"):
        s[n + "_s"] = dma((6,))
        s[n + "_r"] = dma((6,))
    v("REACH", (2, 2, T, 128), BF)
    v("GAINS", (8, HALF), F32)
    v("DNW", (H, D), BF)
    v("M", (4, T, 128), BF)
    v("GA", (8, D), F32)
    for n in ("XF", "COT", "GB", "GF"):
        v(n, (4, T, D) if n != "GF" else (4, 4 * T, W), BF)
        s[n + "_s"] = dma((6,))
        s[n + "_r"] = dma((6,))
    v("N1", (4, T, D), BF)
    v("N2", (4, T, D), BF)
    v("GGS", (4, T, W), BF)
    v("GGR", (4, T, W), BF)
    s["GG_s"] = dma((4,))
    s["GG_r"] = dma((4,))
    v("PR", (5, T + 8, W), F32)
    for n in ("GBV", "GCV", "VAL", "CO", "GCONV"):
        v(n, (4, T, W), F32)
    v("FM", (2, 5, T + 8, W), F32)
    v("HID", (4, T, D), F32)
    v("A", (4, T, H), BF)
    v("GG", (4, T, 2 * H), BF)
    v("GM", (4, T, 3 * W), BF)
    v("OWN", (T, D), F32)
    v("OWNF", (T, D), F32)
    v("OWNB", (T, D), F32)
    for n in ("R2", "R3", "RF"):
        v(n, (2, T, D), BF)
        v(n + "_T", (2, T // 2, D), BF)
        v(n + "_B", (3, T, D), BF)
        s[n + "_s"] = dma((6,))
        s[n + "_r"] = dma((6,))
    v("MIXB", (T, D), BF)
    v("GTB", (T, D), BF)
    v("SM", (8, D), F32)
    for n, rows in (("SE", 16), ("SL", 8)):
        v(n, (rows, 128), F32)
        v(n + "C", (rows, 128), F32)
        for axis in "XYZ":
            v(n + axis, (4, rows, 128), F32)
        s[n + "_s"] = dma((10,))
        s[n + "_r"] = dma((10,))
    s["sw_s"] = dma((10,))
    s["sw_r"] = dma((10,))
    s["ga"] = dma((3,))
    s["w_l"] = dma((4,))
    s["w_s"] = dma((12,))
    s["w_r"] = dma((12,))
    s["halo"] = dma((4,))
    for n, m, k, _ in UNITS:
        v(n + "_W", (2, 4, 4, m, k), BF)
        v(n + "_C", (4, 4, m, k), BF)
        v(n + "_R1", (2, 4, m, k), BF)
        v(n + "_T", (2, 2, m, k), BF)
        v(n + "_S", (4, m, k), BF)
        v(n + "_R2", (3, m, k), BF)
        v(n + "_O", (2, 4, m, k), BF)
        s[n + "_s"] = dma((8,))
        s[n + "_r"] = dma((19,))
        s[n + "_l"] = dma((2,))
    return s


IN_NAMES = ("tok", "cot", "reach", "mgain", "fgain", "ck", "inw", "outw", "guw", "dnw")
OUT_NAMES = ("o_mixed", "o_gt", "o_small", "o_in", "o_out", "o_gu", "o_dn")


class Refs:
    pass


def kernel(*refs):
    q = Refs()
    names = IN_NAMES + OUT_NAMES + tuple(scratch_list())
    for name, ref in zip(names, refs, strict=True):
        setattr(q, name, ref)

    dp = lax.axis_index("dp")
    r = lax.axis_index("row")
    c = lax.axis_index("col")
    yhi = lax.div(dp, 8)
    x = lax.rem(lax.div(dp, 2), 4)
    k = lax.rem(dp, 2)
    y = yhi * 2 + r
    same = k == r
    other = k != r

    def dev(yhi_=None, x_=None, k_=None, r_=None, c_=None):
        yhi_ = yhi if yhi_ is None else yhi_
        x_ = x if x_ is None else x_
        k_ = k if k_ is None else k_
        return {"dp": yhi_ * 8 + x_ * 2 + k_, "row": r if r_ is None else r_, "col": c if c_ is None else c_}

    def at_y(d):
        to = mod(y + d, 4)
        return dev(yhi_=lax.div(to, 2), r_=lax.rem(to, 2))

    def at_x(d):
        return dev(x_=mod(x + d, 4))

    def at_z(d):
        return dev(c_=mod(c + d, 4))

    mate = dev(k_=1 - k)

    def slot_y(d):
        to = mod(y + d, 4)
        return lax.rem(to, 2) * 2 + lax.div(to, 2)

    def rcopy(src, dst, ss, rs, to):
        return pltpu.make_async_remote_copy(
            src_ref=src, dst_ref=dst, send_sem=ss, recv_sem=rs, device_id=to, device_id_type=MESH
        )

    barrier = pltpu.get_barrier_semaphore()
    friends = [mate, dev(r_=1 - r, k_=1 - k)]
    friends += [f(d) for f in (at_x, at_y, at_z) for d in (1, 2, 3)]
    for to in friends:
        pl.semaphore_signal(barrier, inc=1, device_id=to, device_id_type=MESH)

    for n in range(4):
        q.REACH[n // 2, n % 2] = jnp.broadcast_to(q.reach[n : n + 1, :].astype(F32), (T, 128)).T.astype(BF)
    q.GAINS[...] = jnp.zeros((8, HALF), F32)
    q.GAINS[0:1, :] = q.mgain[...]
    q.GAINS[1:2, :] = q.fgain[...]
    pl.semaphore_wait(barrier, len(friends))

    def weight_regions(w):
        if w == 0:
            return (q.inw, q.INW, lambda p, n, a: (q.inw.at[:, pl.ds(p * 128, 128 * n), :], q.INW.at[:, pl.ds(a * HALF + p * 128, 128 * n), :]))
        return (q.dnw, q.DNW, lambda p, n, a: (q.dnw.at[pl.ds(p * 288, 288 * n), :], q.DNW.at[pl.ds(p * 288, 288 * n), pl.ds(pl.multiple_of(a * HALF, HALF), HALF)]))

    def weight_local(w):
        _, _, region = weight_regions(w)
        src, dst = region(0, 4, r)
        return pltpu.make_async_copy(src, dst, q.w_l.at[w])

    def weight_send(w, s):
        _, _, region = weight_regions(w)
        src, dst = region(k * 2 + s, 1, r)
        return rcopy(src, dst, q.w_s.at[w * 3 + s], q.w_r.at[w * 3 + s], at_y(1 - 2 * s))

    def weight_arrival(w, s):
        _, _, region = weight_regions(w)
        src, _ = region(k * 2 + s, 1, r)
        _, dst = region(k * 2 + s, 1, 1 - r)
        return rcopy(src, dst, q.w_s.at[w * 3 + s], q.w_r.at[w * 3 + s], at_y(1 - 2 * s))

    def weight_pass(w, core):
        _, _, region = weight_regions(w)
        _, dst = region(core * 2, 2, 1 - r)
        return rcopy(dst, dst, q.w_s.at[w * 3 + 2], q.w_r.at[w * 3 + 2], mate)

    def weight_start(w):
        for s in (0, 1):
            weight_send(w, s).start()

    def weight_forward(w):
        for s in (0, 1):
            weight_arrival(w, s).wait_recv()
        weight_pass(w, k).start()

    def weight_ready(w):
        weight_local(w).wait()
        weight_pass(w, 1 - k).wait_recv()

    def weight_end(w):
        for s in (0, 1):
            weight_send(w, s).wait_send()
        weight_pass(w, k).wait_send()

    for w in (0, 3):
        weight_local(w).start()

    gu_local = pltpu.make_async_copy(q.guw, q.GUW.at[:, r], q.w_l.at[2])

    def gu_row(s, a):
        h = pl.ds(s * 32, 32)
        return rcopy(q.guw.at[:, x, k, h], q.GUW.at[:, a, x, k, h], q.gu_s.at[s], q.gu_r.at[s], at_y(1 - 2 * s))

    def gu_core(core):
        view = q.GUW.at[:, 1 - r, :, core]
        return rcopy(view, view, q.gu_s.at[2], q.gu_r.at[2], mate)

    gu_local.start()

    half = lambda a: pl.ds(pl.multiple_of(a * HALF, HALF), HALF)
    out_own = q.outw.at[pl.ds(x * 64 + k * 32, 32), :]
    out_local = pltpu.make_async_copy(out_own, q.OUTF.at[c, x, k, :, half(r)], q.o_l.at[0])

    def out_row(a):
        return rcopy(out_own, q.OUTF.at[c, x, k, :, half(a)], q.o_s.at[0], q.o_r.at[0], dev(r_=1 - r))

    def out_col(d, a):
        view = q.OUTF.at[a, x, k]
        return rcopy(view, view, q.o_s.at[d], q.o_r.at[d], at_z(d))

    def out_core(core):
        view = q.OUTF.at[:, :, core]
        return rcopy(view, view, q.o_s.at[7], q.o_r.at[7], mate)

    def out_stage_col():
        out_local.wait()
        out_row(1 - r).wait_recv()
        for d in (1, 3, 2):
            out_col(d, c).start()

    def out_ready():
        out_core(1 - k).wait_recv()
        out_row(r).wait_send()
        for d in (1, 2, 3):
            out_col(d, c).wait_send()
        ring_end(OUX)
        out_core(k).wait_send()

    def gu_ready():
        gu_local.wait()
        gu_core(1 - k).wait_recv()
        for n in (0, 1):
            gu_row(n, r).wait_send()
        ring_end(GUX)
        gu_core(k).wait_send()

    def swap_views(n):
        if n == 0:
            return lambda j: q.tok.at[pl.ds(j * T, T), :], lambda a: q.XF.at[c, :, pl.ds(pl.multiple_of(a * HALF, HALF), HALF)]
        if n == 1:
            return lambda j: q.REACH.at[:, j], lambda a: q.M.at[pl.ds(2 * a, 2)]
        return lambda j: q.cot.at[pl.ds(j * T, T), :], lambda a: q.COT.at[c, :, pl.ds(pl.multiple_of(a * HALF, HALF), HALF)]

    def swap_near(n):
        src, dst = swap_views(n)
        return (
            pltpu.make_async_copy(src(k), dst(r), q.sw_r.at[2 * n]),
            rcopy(src(1 - k), dst(r), q.sw_s.at[2 * n], q.sw_r.at[2 * n], mate),
        )

    def swap_far(n, j):
        src, dst = swap_views(n)
        return rcopy(src(j), dst(r), q.sw_s.at[2 * n + j], q.sw_r.at[2 * n + 1], dev(r_=1 - r, k_=j))

    def swap_start(n):
        @pl.when(same)
        def _():
            near, far = swap_near(n)
            near.start()
            far.start()

        @pl.when(other)
        def _():
            swap_far(n, 0).start()
            swap_far(n, 1).start()

    def swap_wait(n):
        src, dst = swap_views(n)

        @pl.when(same)
        def _():
            near, far = swap_near(n)
            near.wait()
            far.wait_send()

        @pl.when(other)
        def _():
            swap_far(n, 0).wait_send()
            swap_far(n, 1).wait_send()
            rcopy(src(1 - k), dst(r), q.sw_s.at[2 * n], q.sw_r.at[2 * n], mate).wait_recv()

        rcopy(src(0), dst(1 - r), q.sw_s.at[2 * n], q.sw_r.at[2 * n + 1], dev(r_=1 - r)).wait_recv()

    def gain_view(a):
        return q.GA.at[:, pl.ds(pl.multiple_of(a * HALF, HALF), HALF)]

    gain_local = pltpu.make_async_copy(q.GAINS, gain_view(r), q.ga.at[0])
    gain_send = rcopy(q.GAINS, gain_view(r), q.ga.at[1], q.ga.at[2], dev(r_=1 - r))
    gain_take = rcopy(q.GAINS, gain_view(1 - r), q.ga.at[1], q.ga.at[2], dev(r_=1 - r))

    swap_start(0)
    gain_local.start()
    gain_send.start()
    out_local.start()
    out_row(r).start()
    weight_start(0)
    swap_start(1)

    class Ring:
        def __init__(self, name, view, me, target, first=0):
            self.name, self.view, self.me, self.target, self.first = name, view, me, target, first

        def copy(self, n, a):
            view = self.view(a, (0, 1, 1, 0, 0, 1)[n])
            sends, takes = getattr(q, self.name + "_s"), getattr(q, self.name + "_r")
            return rcopy(view, view, sends.at[n], takes.at[self.first + n], self.target(3 if n in (1, 3, 5) else 1))

    def col_view(buf):
        rows = buf.shape[1] // 2
        return lambda a, h: buf.at[a, pl.ds(h * rows, rows)]

    XF = Ring("XF", col_view(q.XF), c, at_z)
    COT = Ring("COT", col_view(q.COT), c, at_z)
    GF = Ring("GF", col_view(q.GF), c, at_z)
    GB = Ring("GB", col_view(q.GB), c, at_z)
    GUX = Ring("GUX", lambda a, h: q.GUW.at[:, 1 - r, a, k, pl.ds(h * 32, 32)], x, at_x)
    OUX = Ring("OUX", lambda a, h: q.OUTF.at[:, a, k, pl.ds(h * 16, 16)], x, at_x)

    def ring_start(ring, parts=(0, 1, 2, 3)):
        for n in parts:
            ring.copy(n, ring.me).start()

    def ring_pass(ring):
        before, after = mod(ring.me - 1, 4), mod(ring.me + 1, 4)
        ring.copy(0, before).wait_recv()
        ring.copy(4, before).start()
        ring.copy(1, after).wait_recv()
        ring.copy(5, after).start()

    def ring_take(ring, d):
        if d == 1:
            ring.copy(2, mod(ring.me - 1, 4)).wait_recv()
        elif d == 3:
            ring.copy(3, mod(ring.me + 1, 4)).wait_recv()
        else:
            ring.copy(4, mod(ring.me + 2, 4)).wait_recv()
            ring.copy(5, mod(ring.me + 2, 4)).wait_recv()

    def ring_end(ring):
        for n in (0, 1, 2, 3):
            ring.copy(n, ring.me).wait_send()
        ring.copy(4, mod(ring.me - 1, 4)).wait_send()
        ring.copy(5, mod(ring.me + 1, 4)).wait_send()

    HT = T // 2

    def reduce_copy(name, n):
        buf, mid, send = getattr(q, name), getattr(q, name + "_T"), getattr(q, name + "_B")
        src, dst, d = (
            (send.at[1, 0:HT], mid.at[0], 1),
            (send.at[1, HT:T], mid.at[1], 3),
            (send.at[0, HT:T], buf.at[0, HT:T], 1),
            (send.at[0, 0:HT], buf.at[0, 0:HT], 1),
            (send.at[2, 0:HT], buf.at[1, 0:HT], 3),
            (send.at[2, HT:T], buf.at[1, HT:T], 3),
        )[n]
        return rcopy(src, dst, getattr(q, name + "_s").at[n], getattr(q, name + "_r").at[n], at_z(d))

    def reduce_sum(name, own):
        buf = getattr(q, name)
        for n in (2, 4, 3, 5):
            reduce_copy(name, n).wait_recv()
        for n in range(6):
            reduce_copy(name, n).wait_send()
        return own[...] + (buf[0].astype(F32) + buf[1].astype(F32))

    def put_part(name, own, e, part):
        mid, send = getattr(q, name + "_T"), getattr(q, name + "_B")
        if e == 0:
            own[...] = part
        elif e == 2:
            send[1] = part.astype(BF)
            reduce_copy(name, 0).start()
            reduce_copy(name, 1).start()
        elif e == 1:
            send[0, HT:T] = part[HT:].astype(BF)
            reduce_copy(name, 2).start()
            reduce_copy(name, 0).wait_recv()
            send[0, 0:HT] = (part[:HT] + mid[0].astype(F32)).astype(BF)
            reduce_copy(name, 3).start()
        else:
            send[2, 0:HT] = part[:HT].astype(BF)
            reduce_copy(name, 4).start()
            reduce_copy(name, 1).wait_recv()
            send[2, HT:T] = (part[HT:] + mid[1].astype(F32)).astype(BF)
            reduce_copy(name, 5).start()

    def two_chunks(ref, pair, lanes=slice(None)):
        return jnp.concatenate([ref[mod(c + e, 4), :, lanes] for e in pair], axis=0)

    def put_pair(name, own, pair, part):
        for n, e in enumerate(pair):
            put_part(name, own, e, part[n * T : (n + 1) * T])

    def arrival(i):
        return i + lax.div(i, 2) - 2 * lax.div(i, 3)

    def norm_scale(value):
        return lax.rsqrt(jnp.sum(value * value, axis=1, keepdims=True) / D + EPS)

    swap_wait(0)
    ring_start(XF)
    for n in (0, 1):
        gu_row(n, r).start()
    swap_start(2)
    out_local.wait()
    out_row(1 - r).wait_recv()
    for d in (1, 3, 2):
        out_col(d, c).start()
    weight_start(3)
    gain_local.wait()
    gain_take.wait_recv()
    weight_forward(0)
    weight_ready(0)

    @pl.when(k == 0)
    def _():
        q.PR[0, 0:8] = jnp.zeros((8, W), F32)

    def in_step(i, carry):
        s = mod(c - arrival(i), 4)

        @pl.when(i == 1)
        def _():
            ring_pass(XF)
            ring_take(XF, 1)

        @pl.when(i == 2)
        def _():
            for d in (1, 3, 2):
                out_col(d, mod(c - d, 4)).wait_recv()
            ring_start(OUX)
            ring_take(XF, 3)

        @pl.when(i == 3)
        def _():
            for n in (0, 1):
                gu_row(n, 1 - r).wait_recv()
            ring_start(GUX)
            ring_take(XF, 2)

        inputs = q.XF[s].astype(F32)
        q.N1[s] = (inputs * norm_scale(inputs) * q.GA[0:1, :]).astype(BF)
        rows = q.N1[s]
        b = dot(rows, q.INW[0])
        v = dot(rows, q.INW[2])
        q.GBV[s] = b
        q.VAL[s] = v
        q.PR[s, 8:] = b * v
        q.GCV[s] = dot(rows, q.INW[1])
        return carry

    lax.fori_loop(0, 4, in_step, 0)
    halo_f = rcopy(q.PR.at[0:4, pl.ds(T, 8)], q.PR.at[pl.ds(k, 4), 0:8], q.halo.at[0], q.halo.at[1], mate)
    halo_ft = rcopy(q.PR.at[0:4, pl.ds(T, 8)], q.PR.at[pl.ds(1 - k, 4), 0:8], q.halo.at[0], q.halo.at[1], mate)
    halo_f.start()
    swap_wait(1)
    halo_f.wait_send()
    halo_ft.wait_recv()

    def masks(s):
        reach = q.M[s].astype(F32)
        first = jnp.where(reach >= 1.0, 1.0, 0.0)
        second = jnp.where(reach >= 2.0, 1.0, 0.0)
        return jnp.concatenate([first, first], axis=1), jnp.concatenate([second, second], axis=1)

    def conv_step(s, carry):
        m1, m2 = masks(s)
        conv = q.ck[0:1, :] * q.PR[s, pl.ds(8, T)]
        conv = conv + q.ck[1:2, :] * q.PR[s, pl.ds(7, T)] * m1
        conv = conv + q.ck[2:3, :] * q.PR[s, pl.ds(6, T)] * m2
        q.CO[s] = conv
        q.GF[c, pl.ds(pl.multiple_of(s * T, T), T)] = (q.GCV[s] * conv).astype(BF)
        return carry

    lax.fori_loop(0, 2, conv_step, 0)
    ring_start(GF, (0, 3))
    lax.fori_loop(2, 4, conv_step, 0)
    ring_start(GF, (1, 2))
    ring_pass(OUX)
    ring_pass(GUX)
    ring_pass(GF)
    swap_wait(2)
    ring_start(COT)
    for d in (1, 3, 2):
        ring_take(OUX, d)
    out_core(k).start()
    weight_forward(3)
    for d in (1, 3, 2):
        ring_take(GUX, d)
    gu_core(k).start()
    for d in (1, 3, 2):
        ring_take(GF, d)
    out_ready()
    gu_ready()
    weight_ready(3)

    def out_step(n, carry):
        lanes = pl.ds(pl.multiple_of(n * HALF, HALF), HALF)
        gated = jnp.concatenate([q.GF[m] for m in range(4)], axis=1)
        branch = dot(gated, q.OUTF[:, :, :, :, lanes].reshape(D, HALF))
        q.HID[:, :, lanes] = q.XF[:, :, lanes].astype(F32) + branch.reshape(4, T, HALF)
        return carry

    lax.fori_loop(0, 2, out_step, 0)

    def norm_step(s, carry):
        hidden = q.HID[s]
        q.N2[s] = (hidden * norm_scale(hidden) * q.GA[1:2, :]).astype(BF)
        return carry

    lax.fori_loop(0, 4, norm_step, 0)

    COLS = ((0, 512), (512, 512), (1024, 128))
    for at, n in COLS:
        rows = q.N2[...].reshape(4 * T, D)
        gate = dot(rows, q.GUW[0, :, :, :, :, at : at + n].reshape(D, n))
        up = dot(rows, q.GUW[1, :, :, :, :, at : at + n].reshape(D, n))
        sig = 1.0 / (1.0 + jnp.exp(-gate))
        silu = gate * sig
        q.A[:, :, at : at + n] = (silu * up).astype(BF).reshape(4, T, n)
        q.GG[:, :, at : at + n] = (up * sig * (1.0 + gate * (1.0 - sig))).astype(BF).reshape(4, T, n)
        q.GG[:, :, H + at : H + at + n] = silu.astype(BF).reshape(4, T, n)
        if at == 0:
            ring_pass(COT)

    def unit(name):
        return next(u for u in UNITS if u[0] == name)

    def g(name, what):
        return getattr(q, name + "_" + what)

    def core_copy(name, core):
        return rcopy(g(name, "W").at[core], g(name, "C"), g(name, "s").at[7], g(name, "r").at[0], mate)

    def first_view(name, d, h):
        w = g(name, "W")
        if unit(name)[3] == 0:
            return w.at[k, pl.ds(2 * h, 2), mod(x + d, 4)]
        return w.at[k, slot_y(d), pl.ds(2 * h, 2)]

    def first_copy(name, n):
        e, h, d = ((2, 0, 1), (2, 1, 3), (1, 1, 1), (1, 0, 1), (3, 0, 3), (3, 1, 3))[n]
        if n < 2:
            dst = g(name, "T").at[h]
        else:
            dst = g(name, "R1").at[e // 2, pl.ds(2 * h, 2)]
        to = at_x(d) if unit(name)[3] == 0 else at_y(d)
        return rcopy(first_view(name, e, h), dst, g(name, "s").at[n], g(name, "r").at[1 + n], to)

    def second_copy(name, d):
        if unit(name)[3] == 0:
            src, to = g(name, "S").at[slot_y(d)], at_y(d)
        else:
            src, to = g(name, "S").at[mod(x + d, 4)], at_x(d)
        return rcopy(src, g(name, "R2").at[d - 1], g(name, "s").at[d - 1], g(name, "r").at[6 + d], to)

    def spread_x(name, d, place):
        view = g(name, "O").at[yhi, place]
        return rcopy(view, view, g(name, "s").at[d - 1], g(name, "r").at[9 + d], at_x(d))

    def ring_x(name):
        return Ring(name, lambda a, h: g(name, "O").at[h, a], x, at_x, 10)

    def spread_y(name, place):
        o = g(name, "O")
        view = o.at[place, x] if unit(name)[3] == 0 else o.at[place]
        return rcopy(view, view, g(name, "s").at[6], g(name, "r").at[16], at_y(2))

    def core_send(name):
        core_copy(name, 1 - k).start()

    def stage_one(name):
        core_copy(name, 1 - k).wait()
        w, other_part = g(name, "W"), g(name, "C")

        def add(i, carry):
            a, b = lax.div(i, 4), lax.rem(i, 4)
            w[k, a, b] = (w[k, a, b].astype(F32) + other_part[a, b].astype(F32)).astype(BF)
            return carry

        lax.fori_loop(0, 16, add, 0)
        for n in (0, 1, 2, 4):
            first_copy(name, n).start()

    def stage_pass(name):
        mid = g(name, "T")
        for n, e, h, last in ((0, 1, 0, 3), (1, 3, 1, 5)):
            first_copy(name, n).wait_recv()
            view = first_view(name, e, h)
            view[...] = (view[...].astype(F32) + mid[h].astype(F32)).astype(BF)
            first_copy(name, last).start()

    def stage_two(name):
        for n in (2, 4, 3, 5):
            first_copy(name, n).wait_recv()
        for n in range(6):
            first_copy(name, n).wait_send()
        w, got, total = g(name, "W"), g(name, "R1"), g(name, "S")

        def add(i, carry):
            mine = w[k, i, x] if unit(name)[3] == 0 else w[k, slot_y(0), i]
            total[i] = (mine.astype(F32) + got[0, i].astype(F32) + got[1, i].astype(F32)).astype(BF)
            return carry

        lax.fori_loop(0, 4, add, 0)
        for d in (1, 3, 2):
            second_copy(name, d).start()

    def stage_three(name):
        for d in (1, 3, 2):
            second_copy(name, d).wait()
        got, total = g(name, "R2"), g(name, "S")
        mine = total[slot_y(0)] if unit(name)[3] == 0 else total[x]
        g(name, "O")[yhi, x] = (mine.astype(F32) + got[0].astype(F32) + got[1].astype(F32) + got[2].astype(F32)).astype(BF)
        if unit(name)[3] == 0:
            spread_y(name, yhi).start()
        else:
            for d in (1, 3, 2):
                spread_x(name, d, x).start()

    def take_x(name):
        for d in (1, 3, 2):
            spread_x(name, d, x).wait_send()
            spread_x(name, d, mod(x - d, 4)).wait_recv()

    def take_y(name):
        spread_y(name, yhi).wait_send()
        spread_y(name, 1 - yhi).wait_recv()

    def stage_four(name):
        if unit(name)[3] == 0:
            take_y(name)
            ring_start(ring_x(name))
        else:
            take_x(name)
            spread_y(name, yhi).start()

    def stage_four_pass(name):
        if unit(name)[3] == 0:
            ring_pass(ring_x(name))

    def results(name, core):
        o = g(name, "O")
        half = unit(name)[3]
        if name in ("dn0", "dn1"):
            at = pl.multiple_of(core * W + half * 128, 128)
            return [(o, q.o_dn.at[:, :, :, pl.ds(at, 128)])]
        if name in ("gt", "up"):
            return [(o, q.o_gu.at[half, core])]
        if name == "oi0":
            at = pl.multiple_of(core * W, W)
            return [(o.at[:, :, :, 0:W], q.o_out.at[:, :, :, pl.ds(at, W)]), (o.at[:, :, :, W:], q.o_in.at[0, core])]
        return [(o.at[:, :, :, 0:W], q.o_in.at[1, core]), (o.at[:, :, :, W:], q.o_in.at[2, core])]

    def stage_five(name):
        if unit(name)[3] == 0:
            for d in (1, 3, 2):
                ring_take(ring_x(name), d)
            ring_end(ring_x(name))
        else:
            take_y(name)
        for n, (src, dst) in enumerate(results(name, k)):
            pltpu.make_async_copy(src, dst, g(name, "l").at[n]).start()
            rcopy(src, dst, g(name, "s").at[n], g(name, "r").at[17 + n], mate).start()

    def stage_six(name):
        for n, (src, dst) in enumerate(results(name, k)):
            pltpu.make_async_copy(src, dst, g(name, "l").at[n]).wait()
            rcopy(src, dst, g(name, "s").at[n], g(name, "r").at[17 + n], mate).wait_send()
        for n, (src, dst) in enumerate(results(name, 1 - k)):
            rcopy(src, dst, g(name, "s").at[n], g(name, "r").at[17 + n], mate).wait_recv()

    def features(ref, a, core):
        at = pl.multiple_of(a * HALF + core * W, W)
        return ref[:, :, pl.ds(at, W)].reshape(4 * T, W)

    def grad_down(core):
        both = jnp.concatenate([features(q.COT, a, core) for a in (0, 1)], axis=1)
        full = dot_tn(q.A[...].reshape(4 * T, H), both).astype(BF).reshape(2, 4, 144, 2 * W)
        for a in (0, 1):
            q.dn0_W[core, 2 * a : 2 * a + 2] = full[:, :, :, a * W : a * W + 128]
            q.dn1_W[core, 2 * a : 2 * a + 2] = full[:, :, :, a * W + 128 : (a + 1) * W]

    def grad_gate_up(core):
        def step(a, carry):
            rows = features(q.N2, a, core)
            q.gt_W[core, pl.ds(2 * a, 2)] = dot_tn(rows, q.GG[:, :, 0:H].reshape(4 * T, H)).astype(BF).reshape(2, 4, 32, H)
            q.up_W[core, pl.ds(2 * a, 2)] = dot_tn(rows, q.GG[:, :, H:].reshape(4 * T, H)).astype(BF).reshape(2, 4, 32, H)
            return carry

        lax.fori_loop(0, 2, step, 0)

    def grad_out_in(core):
        def step(a, carry):
            rows = features(q.N1, a, core)
            gated = q.GF[c]
            q.oi0_W[core, pl.ds(2 * a, 2), :, :, 0:W] = dot_tn(gated, features(q.GB, a, core)).astype(BF).reshape(2, 4, 32, W)
            into = dot_tn(rows, q.GM[...].reshape(4 * T, 3 * W)).astype(BF).reshape(2, 4, 32, 3 * W)
            q.oi0_W[core, pl.ds(2 * a, 2), :, :, W:] = into[:, :, :, 0:W]
            q.oi1_W[core, pl.ds(2 * a, 2)] = into[:, :, :, W:]
            return carry

        lax.fori_loop(0, 2, step, 0)

    def out_pair(pair):
        put_pair("RF", q.OWNF, pair, dot(two_chunks(q.A, pair), q.DNW[...]))

    for d in (1, 3, 2):
        ring_take(COT, d)
    for at, n in COLS:
        ga = dot_nt(q.COT[...].reshape(4 * T, D), q.DNW[at : at + n, :]).reshape(4, T, n)
        for first in (0, H):
            lanes = slice(first + at, first + at + n)
            q.GG[:, :, lanes] = (ga * q.GG[:, :, lanes].astype(F32)).astype(BF)

    def back_pair(pair):
        gate = dot_nt(two_chunks(q.GG, pair, slice(0, H)), q.GUW[0].reshape(D, H))
        up = dot_nt(two_chunks(q.GG, pair, slice(H, 2 * H)), q.GUW[1].reshape(D, H))
        put_pair("R2", q.OWN, pair, gate + up)

    grad_gate_up(1 - k)
    core_send("gt")
    core_send("up")
    back_pair((2, 0))
    grad_gate_up(k)
    stage_one("gt")
    stage_one("up")
    back_pair((1, 3))
    out_pair((2, 0))
    for ring in (XF, GF, COT):
        ring_end(ring)
    grad_down(1 - k)
    core_send("dn0")
    core_send("dn1")
    stage_pass("gt")
    stage_pass("up")
    grad_down(k)
    stage_one("dn0")
    stage_one("dn1")

    def norm_back(value, scale, gain, grad):
        weighted = grad * gain
        inner = jnp.sum(weighted * value, axis=1, keepdims=True)
        back = scale * weighted - value * (scale * scale * scale) * inner / D
        return back, jnp.sum(grad * value * scale, axis=0, keepdims=True)

    grad_normed = reduce_sum("R2", q.OWN)
    hidden = q.HID[c]
    back, grad_gain = norm_back(hidden, norm_scale(hidden), q.GA[1:2, :], grad_normed)
    q.SM[...] = jnp.zeros((8, D), F32)
    q.SM[1:2, :] = grad_gain
    grad_hidden = q.COT[c].astype(F32) + back
    q.GB[c] = grad_hidden.astype(BF)
    q.OWN[...] = grad_hidden
    grad_gated = dot_nt(q.GB[c], q.OUTF[...].reshape(D, D)).astype(BF)
    for n in range(4):
        q.GGS[n] = grad_gated[:, n * W : (n + 1) * W]

    def gated_copy(d, dst):
        return rcopy(q.GGS.at[mod(c + d, 4)], q.GGR.at[dst], q.GG_s.at[d], q.GG_r.at[d], at_z(d))

    for d in (1, 3, 2):
        gated_copy(d, c).start()
    ring_start(GB)
    q.GGR[c] = q.GGS[c]
    stage_two("gt")
    stage_two("up")
    stage_pass("dn0")
    stage_pass("dn1")

    def home(n):
        buf, out = ((q.MIXB, q.o_mixed), (q.GTB, q.o_gt))[n]
        base = 6 + 2 * n
        halves = lambda a: buf.at[:, pl.ds(pl.multiple_of(a * HALF, HALF), HALF)]
        rows = lambda j: out.at[pl.ds(j * T, T), :]
        near_local = pltpu.make_async_copy(halves(r), rows(k), q.sw_r.at[base])
        near_far = rcopy(halves(r), rows(k), q.sw_s.at[base], q.sw_r.at[base + 1], mate)
        away = rcopy(halves(1 - r), rows(k), q.sw_s.at[base + 1], q.sw_r.at[base + k], dev(r_=1 - r, k_=r))
        return halves, rows, base, near_local, near_far, away

    def home_start(n):
        halves, rows, base, near_local, near_far, away = home(n)

        @pl.when(same)
        def _():
            near_local.start()

        @pl.when(other)
        def _():
            near_far.start()

        away.start()

    def home_wait(n):
        halves, rows, base, near_local, near_far, away = home(n)

        @pl.when(same)
        def _():
            near_local.wait()
            rcopy(halves(r), rows(1 - k), q.sw_s.at[base], q.sw_r.at[base + 1], mate).wait_recv()

        @pl.when(other)
        def _():
            near_far.wait_send()
            for j in (0, 1):
                rcopy(halves(r), rows(j), q.sw_s.at[base], q.sw_r.at[base + j], dev(r_=1 - r)).wait_recv()

        away.wait_send()

    @pl.when(k == 1)
    def _():
        q.FM[0, 4, pl.ds(T, 8)] = jnp.zeros((8, W), F32)
        q.FM[1, 4, pl.ds(T, 8)] = jnp.zeros((8, W), F32)

    for d in (1, 3, 2):
        gated_copy(d, c).wait_send()
        gated_copy(d, mod(c - d, 4)).wait_recv()

    def conv_back_step(s, carry):
        grad_gated = q.GGR[s].astype(F32)
        q.GM[s, :, W : 2 * W] = (grad_gated * q.CO[s]).astype(BF)
        grad_conv = grad_gated * q.GCV[s]
        q.GCONV[s] = grad_conv
        m1, m2 = masks(s)
        q.FM[0, s + 1, 0:T] = grad_conv * m1
        q.FM[1, s + 1, 0:T] = grad_conv * m2
        return carry

    lax.fori_loop(0, 4, conv_back_step, 0)
    halo_b = rcopy(q.FM.at[:, 1:5, 0:8], q.FM.at[:, pl.ds(k, 4), pl.ds(T, 8)], q.halo.at[2], q.halo.at[3], mate)
    halo_bt = rcopy(q.FM.at[:, 1:5, 0:8], q.FM.at[:, pl.ds(1 - k, 4), pl.ds(T, 8)], q.halo.at[2], q.halo.at[3], mate)
    halo_b.start()
    stage_two("dn0")
    stage_two("dn1")
    ring_pass(GB)
    halo_b.wait_send()
    halo_bt.wait_recv()

    def product_back_step(s, carry):
        grad_conv = q.GCONV[s]
        grad_product = q.ck[0:1, :] * grad_conv
        grad_product = grad_product + q.ck[1:2, :] * q.FM[0, s + 1, pl.ds(1, T)]
        grad_product = grad_product + q.ck[2:3, :] * q.FM[1, s + 1, pl.ds(2, T)]
        q.SM[2:3, 0:W] += jnp.sum(grad_conv * q.PR[s, pl.ds(8, T)], axis=0, keepdims=True)
        q.SM[3:4, 0:W] += jnp.sum(q.FM[0, s + 1, pl.ds(0, T)] * q.PR[s, pl.ds(7, T)], axis=0, keepdims=True)
        q.SM[4:5, 0:W] += jnp.sum(q.FM[1, s + 1, pl.ds(0, T)] * q.PR[s, pl.ds(6, T)], axis=0, keepdims=True)
        q.GM[s, :, 0:W] = (grad_product * q.VAL[s]).astype(BF)
        q.GM[s, :, 2 * W :] = (grad_product * q.GBV[s]).astype(BF)
        return carry

    lax.fori_loop(0, 4, product_back_step, 0)

    def in_pair(pair):
        part = [dot_nt(two_chunks(q.GM, pair, slice(n * W, (n + 1) * W)), q.INW[n]) for n in range(3)]
        put_pair("R3", q.OWNB, pair, part[0] + part[1] + part[2])

    class Small:
        def __init__(self, name):
            self.name = name
            self.own, self.other = getattr(q, name), getattr(q, name + "C")
            self.axes = [(getattr(q, name + axis), me, at) for axis, me, at in (("X", x, at_x), ("Y", y, at_y), ("Z", c, at_z))]
            self.sends, self.takes = getattr(q, name + "_s"), getattr(q, name + "_r")

        def core(self):
            return rcopy(self.own, self.other, self.sends.at[9], self.takes.at[9], mate)

        def copy(self, n, d, a):
            buf, _, to = self.axes[n]
            return rcopy(buf.at[a], buf.at[a], self.sends.at[3 * n + d - 1], self.takes.at[3 * n + d - 1], to(d))

        def take(self, n):
            buf, me, _ = self.axes[n]
            for d in (1, 2, 3):
                self.copy(n, d, me).wait_send()
                self.copy(n, d, mod(me - d, 4)).wait_recv()
            return (buf[0] + buf[1]) + (buf[2] + buf[3])

        def step(self, n):
            if n == 0:
                self.core().wait()
                value = self.own[...] + self.other[...]
            else:
                value = self.take(n - 1)
            self.own[...] = value
            buf, me, _ = self.axes[n]
            buf[me] = value
            for d in (1, 2, 3):
                self.copy(n, d, me).start()

    early, late = Small("SE"), Small("SL")
    for n in range(8):
        q.SE[n : n + 1, :] = q.SM[1:2, n * 128 : (n + 1) * 128]
    for n in range(8):
        q.SE[8 + n : 9 + n, :] = q.SM[2 + n // 2 : 3 + n // 2, (n % 2) * 128 : (n % 2 + 1) * 128]
    early.core().start()
    in_pair((2, 0))
    stage_three("gt")
    stage_three("up")
    in_pair((1, 3))
    early.step(0)
    for d in (1, 3, 2):
        ring_take(GB, d)
    grad_out_in(1 - k)
    core_send("oi0")
    core_send("oi1")
    stage_four("gt")
    stage_four("up")
    grad_out_in(k)
    ring_end(GB)
    stage_one("oi0")
    stage_one("oi1")
    early.step(1)
    out_pair((1, 3))
    stage_three("dn0")
    stage_three("dn1")
    stage_pass("oi0")
    stage_pass("oi1")
    stage_four_pass("gt")
    early.step(2)
    stage_four("dn0")
    stage_four("dn1")
    grad_normed = reduce_sum("R3", q.OWNB)
    inputs = q.XF[c].astype(F32)
    back, grad_gain = norm_back(inputs, norm_scale(inputs), q.GA[0:1, :], grad_normed)
    for n in range(8):
        q.SL[n : n + 1, :] = grad_gain[:, n * 128 : (n + 1) * 128]
    late.core().start()
    q.GTB[...] = (q.OWN[...] + back).astype(BF)
    home_start(1)
    stage_two("oi0")
    stage_two("oi1")
    late.step(0)
    stage_five("gt")
    stage_five("up")
    stage_four_pass("dn0")
    late.step(1)
    stage_three("oi0")
    stage_three("oi1")
    q.MIXB[...] = (q.HID[c] + reduce_sum("RF", q.OWNF)).astype(BF)
    home_start(0)
    late.step(2)
    stage_five("dn0")
    stage_five("dn1")
    stage_four("oi0")
    stage_four("oi1")
    stage_four_pass("oi0")
    early_gain = early.take(2)
    late_gain = late.take(2)
    q.SL[...] = late_gain
    q.SEC[0:8, :] = early_gain[0:8, :]
    q.o_small[...] = jnp.zeros((8, HALF), F32)
    for n in range(4):
        lanes = slice(n * 128, (n + 1) * 128)
        q.o_small[0:1, lanes] = q.SL[pl.ds(r * 4 + n, 1), :]
        q.o_small[1:2, lanes] = q.SEC[pl.ds(r * 4 + n, 1), :]
    for n in range(6):
        q.o_small[2 + n // 2 : 3 + n // 2, (n % 2) * 128 : (n % 2 + 1) * 128] = q.SE[8 + n : 9 + n, :]
    stage_five("oi0")
    stage_five("oi1")
    home_wait(0)
    home_wait(1)
    gain_send.wait_send()
    for w in (0, 3):
        weight_end(w)
    for name in ("dn0", "dn1", "gt", "up", "oi0", "oi1"):
        stage_six(name)


def cast_kernel(mixed, tokens, small, g_in, g_out, g_gu, g_dn, o_mixed, o_tokens, o_mixer, o_kernel, o_ffn, o_in, o_out, o_gu, o_dn):
    o_mixed[...] = mixed[...]
    o_mixer[...] = small[0:1, :]
    o_ffn[...] = small[1:2, :]
    o_kernel[...] = small[2:5, 0:W]
    for src, dst in ((tokens, o_tokens), (g_in, o_in), (g_out, o_out), (g_gu, o_gu), (g_dn, o_dn)):
        dst[...] = src[...].astype(F32)


def cast_all(*arrays):
    steps = 8

    def cut(shape):
        at = len(shape) - 2
        block = shape[:at] + (shape[at] // steps, shape[-1])
        return pl.BlockSpec(block, lambda i: (0,) * at + (i, 0))

    def whole(shape):
        return pl.BlockSpec(shape, lambda i: (0, 0))

    specs = [whole(a.shape) if n == 2 else cut(a.shape) for n, a in enumerate(arrays)]
    small = [(1, HALF), (3, W), (1, HALF)]
    kinds = [BF] + [F32] * 5
    big = [cut(a.shape) for n, a in enumerate(arrays) if n != 2]
    shapes = [jax.ShapeDtypeStruct(a.shape, kind) for a, kind in zip([a for n, a in enumerate(arrays) if n != 2], kinds)]
    return pl.pallas_call(
        cast_kernel,
        grid=(steps,),
        in_specs=specs,
        out_specs=big[:2] + [whole(n) for n in small] + big[2:],
        out_shape=shapes[:2] + [jax.ShapeDtypeStruct(n, F32) for n in small] + shapes[2:],
        compiler_params=pltpu.CompilerParams(vmem_limit_bytes=60 * 2**20),
        name="cast_all",
    )(*arrays)


def per_device(
    tokens,
    mixer_gain,
    in_weight,
    conv_kernel,
    out_weight,
    ffn_gain,
    gate_up_weight,
    down_weight,
    conv_reach,
    cotangent,
):
    hbm = pl.BlockSpec(memory_space=pl.ANY)
    vmem = pl.BlockSpec(memory_space=pltpu.VMEM)
    mixed, grad_tokens, small, g_in, g_out, g_gu, g_dn = pl.pallas_call(
        kernel,
        out_shape=(
            jax.ShapeDtypeStruct((2 * T, HALF), BF),
            jax.ShapeDtypeStruct((2 * T, HALF), BF),
            jax.ShapeDtypeStruct((8, HALF), F32),
            jax.ShapeDtypeStruct((3, 2, 2, 4, 32, W), BF),
            jax.ShapeDtypeStruct((2, 4, 32, HALF), BF),
            jax.ShapeDtypeStruct((2, 2, 2, 4, 32, H), BF),
            jax.ShapeDtypeStruct((2, 4, 144, HALF), BF),
        ),
        in_specs=[hbm, hbm, vmem, vmem, vmem, vmem, hbm, hbm, hbm, hbm],
        out_specs=(hbm, hbm, vmem, hbm, hbm, hbm, hbm),
        scratch_shapes=list(scratch_list().values()),
        compiler_params=pltpu.CompilerParams(
            collective_id=0, has_side_effects=True, vmem_limit_bytes=60 * 2**20
        ),
        name="block_step",
    )(
        tokens,
        cotangent,
        conv_reach.reshape(4, T),
        mixer_gain.reshape(1, HALF),
        ffn_gain.reshape(1, HALF),
        conv_kernel,
        in_weight,
        out_weight,
        gate_up_weight.reshape(2, 4, 2, 64, H),
        down_weight,
    )
    results = cast_all(
        mixed,
        grad_tokens,
        small,
        g_in.reshape(3, HALF, W),
        g_out.reshape(W, HALF),
        g_gu.reshape(2, HALF, H),
        g_dn.reshape(H, HALF),
    )
    mixed, grad_tokens, mixer, kernel_grad, ffn, g_in, g_out, g_gu, g_dn = results
    return (mixed, grad_tokens, mixer.reshape(HALF), g_in, kernel_grad, g_out, ffn.reshape(HALF), g_gu, g_dn)


def solution(mesh):
    return jax.shard_map(
        per_device,
        mesh=mesh,
        in_specs=(
            P(("dp", "col"), "row"),
            P("row"),
            P(None, "row", "col"),
            P(None, "col"),
            P("col", "row"),
            P("row"),
            P(None, "row", "col"),
            P("col", "row"),
            P(("dp", "row")),
            P(("dp", "col"), "row"),
        ),
        out_specs=(
            P(("dp", "col"), "row"),
            P(("dp", "col"), "row"),
            P("row"),
            P(None, "row", "col"),
            P(None, "col"),
            P("col", "row"),
            P("row"),
            P(None, "row", "col"),
            P("col", "row"),
        ),
        check_vma=False,
    )
```

```python
import functools

import jax
import jax.numpy as jnp
from jax import lax
from jax.experimental import pallas as pl
from jax.experimental.pallas import tpu as pltpu
from jax.sharding import PartitionSpec as P

MESH = pl.DeviceIdType.MESH
D = 1024
HALF = 512
T = 128
W = 256
H = 1152
EPS = 1e-05
F32 = jnp.float32
BF = jnp.bfloat16

UNITS = (("dn0", 144, 128, 0), ("dn1", 144, 128, 1), ("gt", 32, H, 0), ("up", 32, H, 1), ("oi0", 32, 512, 0), ("oi1", 32, 512, 1))


def mod(a, n):
    return lax.rem(a + 4 * n, n)


def dot(a, b):
    return lax.dot_general(a, b, (((1,), (0,)), ((), ())), preferred_element_type=F32)


def dot_nt(a, b):
    return lax.dot_general(a, b, (((1,), (1,)), ((), ())), preferred_element_type=F32)


def dot_tn(a, b):
    return lax.dot_general(a, b, (((0,), (0,)), ((), ())), preferred_element_type=F32)


def scratch_list():
    s = {}
    dma = pltpu.SemaphoreType.DMA

    def v(name, shape, dtype):
        s[name] = pltpu.VMEM(shape, dtype)

    v("INW", (3, D, W), BF)
    v("OUTF", (4, 4, 2, 32, D), BF)
    s["o_s"] = dma((8,))
    s["o_r"] = dma((8,))
    s["o_l"] = dma((1,))
    v("GUW", (2, 2, 4, 2, 64, H), BF)
    s["gu_s"] = dma((3,))
    s["gu_r"] = dma((3,))
    for n in ("GUX", "OUX"):
        s[n + "_s"] = dma((6,))
        s[n + "_r"] = dma((6,))
    v("REACH", (2, 2, T, 128), BF)
    v("GAINS", (8, HALF), F32)
    v("DNW", (H, D), BF)
    v("M", (4, T, 128), BF)
    v("GA", (8, D), F32)
    for n in ("XF", "COT", "GB", "GF"):
        v(n, (4, T, D) if n != "GF" else (4, 4 * T, W), BF)
        s[n + "_s"] = dma((6,))
        s[n + "_r"] = dma((6,))
    v("N1", (4, T, D), BF)
    v("N2", (4, T, D), BF)
    v("GGS", (4, T, W), BF)
    v("GGR", (4, T, W), BF)
    s["GG_s"] = dma((4,))
    s["GG_r"] = dma((4,))
    v("PR", (5, T + 8, W), F32)
    for n in ("GBV", "GCV", "VAL", "CO", "GCONV"):
        v(n, (4, T, W), F32)
    v("FM", (2, 5, T + 8, W), F32)
    v("HID", (4, T, D), F32)
    v("A", (4, T, H), BF)
    v("GG", (4, T, 2 * H), BF)
    v("GM", (4, T, 3 * W), BF)
    v("OWN", (T, D), F32)
    v("OWNF", (T, D), F32)
    v("OWNB", (T, D), F32)
    for n in ("R2", "R3", "RF"):
        v(n, (2, T, D), BF)
        v(n + "_T", (2, T // 2, D), BF)
        v(n + "_B", (3, T, D), BF)
        s[n + "_s"] = dma((6,))
        s[n + "_r"] = dma((6,))
    v("MIXB", (T, D), BF)
    v("GTB", (T, D), BF)
    v("SM", (8, D), F32)
    for n, rows in (("SE", 16), ("SL", 8)):
        v(n, (rows, 128), F32)
        v(n + "C", (rows, 128), F32)
        for axis in "XYZ":
            v(n + axis, (4, rows, 128), F32)
        s[n + "_s"] = dma((10,))
        s[n + "_r"] = dma((10,))
    s["sw_s"] = dma((10,))
    s["sw_r"] = dma((10,))
    s["ga"] = dma((3,))
    s["w_l"] = dma((4,))
    s["w_s"] = dma((12,))
    s["w_r"] = dma((12,))
    s["halo"] = dma((4,))
    for n, m, k, _ in UNITS:
        v(n + "_W", (2, 4, 4, m, k), BF)
        v(n + "_C", (4, 4, m, k), BF)
        v(n + "_R1", (2, 4, m, k), BF)
        v(n + "_T", (2, 2, m, k), BF)
        v(n + "_S", (4, m, k), BF)
        v(n + "_R2", (3, m, k), BF)
        v(n + "_O", (2, 4, m, k), BF)
        s[n + "_s"] = dma((8,))
        s[n + "_r"] = dma((19,))
        s[n + "_l"] = dma((2,))
    return s


IN_NAMES = ("tok", "cot", "reach", "mgain", "fgain", "ck", "inw", "outw", "guw", "dnw")
OUT_NAMES = ("o_mixed", "o_gt", "o_small", "o_in", "o_out", "o_gu", "o_dn")


class Refs:
    pass


def kernel(*refs):
    q = Refs()
    names = IN_NAMES + OUT_NAMES + tuple(scratch_list())
    for name, ref in zip(names, refs, strict=True):
        setattr(q, name, ref)

    dp = lax.axis_index("dp")
    r = lax.axis_index("row")
    c = lax.axis_index("col")
    yhi = lax.div(dp, 8)
    x = lax.rem(lax.div(dp, 2), 4)
    k = lax.rem(dp, 2)
    y = yhi * 2 + r
    same = k == r
    other = k != r

    def dev(yhi_=None, x_=None, k_=None, r_=None, c_=None):
        yhi_ = yhi if yhi_ is None else yhi_
        x_ = x if x_ is None else x_
        k_ = k if k_ is None else k_
        return {"dp": yhi_ * 8 + x_ * 2 + k_, "row": r if r_ is None else r_, "col": c if c_ is None else c_}

    def at_y(d):
        to = mod(y + d, 4)
        return dev(yhi_=lax.div(to, 2), r_=lax.rem(to, 2))

    def at_x(d):
        return dev(x_=mod(x + d, 4))

    def at_z(d):
        return dev(c_=mod(c + d, 4))

    mate = dev(k_=1 - k)

    def slot_y(d):
        to = mod(y + d, 4)
        return lax.rem(to, 2) * 2 + lax.div(to, 2)

    def rcopy(src, dst, ss, rs, to):
        return pltpu.make_async_remote_copy(
            src_ref=src, dst_ref=dst, send_sem=ss, recv_sem=rs, device_id=to, device_id_type=MESH
        )

    barrier = pltpu.get_barrier_semaphore()
    friends = [mate, dev(r_=1 - r, k_=1 - k)]
    friends += [f(d) for f in (at_x, at_y, at_z) for d in (1, 2, 3)]
    for to in friends:
        pl.semaphore_signal(barrier, inc=1, device_id=to, device_id_type=MESH)

    for n in range(4):
        q.REACH[n // 2, n % 2] = jnp.broadcast_to(q.reach[n : n + 1, :].astype(F32), (T, 128)).T.astype(BF)
    q.GAINS[...] = jnp.zeros((8, HALF), F32)
    q.GAINS[0:1, :] = q.mgain[...]
    q.GAINS[1:2, :] = q.fgain[...]
    pl.semaphore_wait(barrier, len(friends))

    def weight_regions(w):
        if w == 0:
            return (q.inw, q.INW, lambda p, n, a: (q.inw.at[:, pl.ds(p * 128, 128 * n), :], q.INW.at[:, pl.ds(a * HALF + p * 128, 128 * n), :]))
        return (q.dnw, q.DNW, lambda p, n, a: (q.dnw.at[pl.ds(p * 288, 288 * n), :], q.DNW.at[pl.ds(p * 288, 288 * n), pl.ds(pl.multiple_of(a * HALF, HALF), HALF)]))

    def weight_local(w):
        _, _, region = weight_regions(w)
        src, dst = region(0, 4, r)
        return pltpu.make_async_copy(src, dst, q.w_l.at[w])

    def weight_send(w, s):
        _, _, region = weight_regions(w)
        src, dst = region(k * 2 + s, 1, r)
        return rcopy(src, dst, q.w_s.at[w * 3 + s], q.w_r.at[w * 3 + s], at_y(1 - 2 * s))

    def weight_arrival(w, s):
        _, _, region = weight_regions(w)
        src, _ = region(k * 2 + s, 1, r)
        _, dst = region(k * 2 + s, 1, 1 - r)
        return rcopy(src, dst, q.w_s.at[w * 3 + s], q.w_r.at[w * 3 + s], at_y(1 - 2 * s))

    def weight_pass(w, core):
        _, _, region = weight_regions(w)
        _, dst = region(core * 2, 2, 1 - r)
        return rcopy(dst, dst, q.w_s.at[w * 3 + 2], q.w_r.at[w * 3 + 2], mate)

    def weight_start(w):
        for s in (0, 1):
            weight_send(w, s).start()

    def weight_forward(w):
        for s in (0, 1):
            weight_arrival(w, s).wait_recv()
        weight_pass(w, k).start()

    def weight_ready(w):
        weight_local(w).wait()
        weight_pass(w, 1 - k).wait_recv()

    def weight_end(w):
        for s in (0, 1):
            weight_send(w, s).wait_send()
        weight_pass(w, k).wait_send()

    for w in (0, 3):
        weight_local(w).start()

    gu_local = pltpu.make_async_copy(q.guw, q.GUW.at[:, r], q.w_l.at[2])

    def gu_row(s, a):
        h = pl.ds(s * 32, 32)
        return rcopy(q.guw.at[:, x, k, h], q.GUW.at[:, a, x, k, h], q.gu_s.at[s], q.gu_r.at[s], at_y(1 - 2 * s))

    def gu_core(core):
        view = q.GUW.at[:, 1 - r, :, core]
        return rcopy(view, view, q.gu_s.at[2], q.gu_r.at[2], mate)

    gu_local.start()

    half = lambda a: pl.ds(pl.multiple_of(a * HALF, HALF), HALF)
    out_own = q.outw.at[pl.ds(x * 64 + k * 32, 32), :]
    out_local = pltpu.make_async_copy(out_own, q.OUTF.at[c, x, k, :, half(r)], q.o_l.at[0])

    def out_row(a):
        return rcopy(out_own, q.OUTF.at[c, x, k, :, half(a)], q.o_s.at[0], q.o_r.at[0], dev(r_=1 - r))

    def out_col(d, a):
        view = q.OUTF.at[a, x, k]
        return rcopy(view, view, q.o_s.at[d], q.o_r.at[d], at_z(d))

    def out_core(core):
        view = q.OUTF.at[:, :, core]
        return rcopy(view, view, q.o_s.at[7], q.o_r.at[7], mate)

    def out_stage_col():
        out_local.wait()
        out_row(1 - r).wait_recv()
        for d in (1, 3, 2):
            out_col(d, c).start()

    def out_ready():
        out_core(1 - k).wait_recv()
        out_row(r).wait_send()
        for d in (1, 2, 3):
            out_col(d, c).wait_send()
        ring_end(OUX)
        out_core(k).wait_send()

    def gu_ready():
        gu_local.wait()
        gu_core(1 - k).wait_recv()
        for n in (0, 1):
            gu_row(n, r).wait_send()
        ring_end(GUX)
        gu_core(k).wait_send()

    def swap_views(n):
        if n == 0:
            return lambda j: q.tok.at[pl.ds(j * T, T), :], lambda a: q.XF.at[c, :, pl.ds(pl.multiple_of(a * HALF, HALF), HALF)]
        if n == 1:
            return lambda j: q.REACH.at[:, j], lambda a: q.M.at[pl.ds(2 * a, 2)]
        return lambda j: q.cot.at[pl.ds(j * T, T), :], lambda a: q.COT.at[c, :, pl.ds(pl.multiple_of(a * HALF, HALF), HALF)]

    def swap_near(n):
        src, dst = swap_views(n)
        return (
            pltpu.make_async_copy(src(k), dst(r), q.sw_r.at[2 * n]),
            rcopy(src(1 - k), dst(r), q.sw_s.at[2 * n], q.sw_r.at[2 * n], mate),
        )

    def swap_far(n, j):
        src, dst = swap_views(n)
        return rcopy(src(j), dst(r), q.sw_s.at[2 * n + j], q.sw_r.at[2 * n + 1], dev(r_=1 - r, k_=j))

    def swap_start(n):
        @pl.when(same)
        def _():
            near, far = swap_near(n)
            near.start()
            far.start()

        @pl.when(other)
        def _():
            swap_far(n, 0).start()
            swap_far(n, 1).start()

    def swap_wait(n):
        src, dst = swap_views(n)

        @pl.when(same)
        def _():
            near, far = swap_near(n)
            near.wait()
            far.wait_send()

        @pl.when(other)
        def _():
            swap_far(n, 0).wait_send()
            swap_far(n, 1).wait_send()
            rcopy(src(1 - k), dst(r), q.sw_s.at[2 * n], q.sw_r.at[2 * n], mate).wait_recv()

        rcopy(src(0), dst(1 - r), q.sw_s.at[2 * n], q.sw_r.at[2 * n + 1], dev(r_=1 - r)).wait_recv()

    def gain_view(a):
        return q.GA.at[:, pl.ds(pl.multiple_of(a * HALF, HALF), HALF)]

    gain_local = pltpu.make_async_copy(q.GAINS, gain_view(r), q.ga.at[0])
    gain_send = rcopy(q.GAINS, gain_view(r), q.ga.at[1], q.ga.at[2], dev(r_=1 - r))
    gain_take = rcopy(q.GAINS, gain_view(1 - r), q.ga.at[1], q.ga.at[2], dev(r_=1 - r))

    swap_start(0)
    gain_local.start()
    gain_send.start()
    out_local.start()
    out_row(r).start()

    class Ring:
        def __init__(self, name, view, me, target, first=0):
            self.name, self.view, self.me, self.target, self.first = name, view, me, target, first

        def copy(self, n, a):
            view = self.view(a, (0, 1, 1, 0, 0, 1)[n])
            sends, takes = getattr(q, self.name + "_s"), getattr(q, self.name + "_r")
            return rcopy(view, view, sends.at[n], takes.at[self.first + n], self.target(3 if n in (1, 3, 5) else 1))

    def col_view(buf):
        rows = buf.shape[1] // 2
        return lambda a, h: buf.at[a, pl.ds(h * rows, rows)]

    XF = Ring("XF", col_view(q.XF), c, at_z)
    COT = Ring("COT", col_view(q.COT), c, at_z)
    GF = Ring("GF", col_view(q.GF), c, at_z)
    GB = Ring("GB", col_view(q.GB), c, at_z)
    GUX = Ring("GUX", lambda a, h: q.GUW.at[:, 1 - r, a, k, pl.ds(h * 32, 32)], x, at_x)
    OUX = Ring("OUX", lambda a, h: q.OUTF.at[:, a, k, pl.ds(h * 16, 16)], x, at_x)

    def ring_start(ring, parts=(0, 1, 2, 3)):
        for n in parts:
            ring.copy(n, ring.me).start()

    def ring_pass(ring):
        before, after = mod(ring.me - 1, 4), mod(ring.me + 1, 4)
        ring.copy(0, before).wait_recv()
        ring.copy(4, before).start()
        ring.copy(1, after).wait_recv()
        ring.copy(5, after).start()

    def ring_take(ring, d):
        if d == 1:
            ring.copy(2, mod(ring.me - 1, 4)).wait_recv()
        elif d == 3:
            ring.copy(3, mod(ring.me + 1, 4)).wait_recv()
        else:
            ring.copy(4, mod(ring.me + 2, 4)).wait_recv()
            ring.copy(5, mod(ring.me + 2, 4)).wait_recv()

    def ring_end(ring):
        for n in (0, 1, 2, 3):
            ring.copy(n, ring.me).wait_send()
        ring.copy(4, mod(ring.me - 1, 4)).wait_send()
        ring.copy(5, mod(ring.me + 1, 4)).wait_send()

    HT = T // 2

    def reduce_copy(name, n):
        buf, mid, send = getattr(q, name), getattr(q, name + "_T"), getattr(q, name + "_B")
        src, dst, d = (
            (send.at[1, 0:HT], mid.at[0], 1),
            (send.at[1, HT:T], mid.at[1], 3),
            (send.at[0, HT:T], buf.at[0, HT:T], 1),
            (send.at[0, 0:HT], buf.at[0, 0:HT], 1),
            (send.at[2, 0:HT], buf.at[1, 0:HT], 3),
            (send.at[2, HT:T], buf.at[1, HT:T], 3),
        )[n]
        return rcopy(src, dst, getattr(q, name + "_s").at[n], getattr(q, name + "_r").at[n], at_z(d))

    def reduce_sum(name, own):
        buf = getattr(q, name)
        for n in (2, 4, 3, 5):
            reduce_copy(name, n).wait_recv()
        for n in range(6):
            reduce_copy(name, n).wait_send()
        return own[...] + (buf[0].astype(F32) + buf[1].astype(F32))

    def put_part(name, own, e, part):
        mid, send = getattr(q, name + "_T"), getattr(q, name + "_B")
        if e == 0:
            own[...] = part
        elif e == 2:
            send[1] = part.astype(BF)
            reduce_copy(name, 0).start()
            reduce_copy(name, 1).start()

    def put_last(name, before, after):
        mid, send = getattr(q, name + "_T"), getattr(q, name + "_B")
        send[0, HT:T] = before[HT:].astype(BF)
        reduce_copy(name, 2).start()
        send[2, 0:HT] = after[:HT].astype(BF)
        reduce_copy(name, 4).start()
        reduce_copy(name, 0).wait_recv()
        send[0, 0:HT] = (before[:HT] + mid[0].astype(F32)).astype(BF)
        reduce_copy(name, 3).start()
        reduce_copy(name, 1).wait_recv()
        send[2, HT:T] = (after[HT:] + mid[1].astype(F32)).astype(BF)
        reduce_copy(name, 5).start()

    def two_chunks(ref, pair, lanes=slice(None)):
        return jnp.concatenate([ref[mod(c + e, 4), :, lanes] for e in pair], axis=0)

    def put_pair(name, own, pair, part):
        if pair == (1, 3):
            put_last(name, part[:T], part[T:])
        else:
            for n, e in enumerate(pair):
                put_part(name, own, e, part[n * T : (n + 1) * T])

    def arrival(i):
        return i + lax.div(i, 2) - 2 * lax.div(i, 3)

    def norm_scale(value):
        return lax.rsqrt(jnp.sum(value * value, axis=1, keepdims=True) / D + EPS)

    swap_wait(0)
    ring_start(XF)
    weight_start(0)
    out_local.wait()
    out_row(1 - r).wait_recv()
    for d in (1, 3, 2):
        out_col(d, c).start()
    gain_local.wait()
    gain_take.wait_recv()
    weight_forward(0)
    for n in (0, 1):
        gu_row(n, r).start()
    swap_start(1)
    swap_start(2)
    weight_ready(0)

    @pl.when(k == 0)
    def _():
        q.PR[0, 0:8] = jnp.zeros((8, W), F32)

    def in_step(i, carry):
        s = mod(c - arrival(i), 4)

        @pl.when(i == 1)
        def _():
            ring_pass(XF)
            for d in (1, 3, 2):
                out_col(d, mod(c - d, 4)).wait_recv()
            ring_start(OUX)
            ring_take(XF, 1)

        @pl.when(i == 2)
        def _():
            ring_take(XF, 3)
            for n in (0, 1):
                gu_row(n, 1 - r).wait_recv()
            ring_start(GUX)

        @pl.when(i == 3)
        def _():
            ring_take(XF, 2)

        inputs = q.XF[s].astype(F32)
        q.N1[s] = (inputs * norm_scale(inputs) * q.GA[0:1, :]).astype(BF)
        rows = q.N1[s]
        b = dot(rows, q.INW[0])
        v = dot(rows, q.INW[2])
        q.GBV[s] = b
        q.VAL[s] = v
        q.PR[s, 8:] = b * v
        q.GCV[s] = dot(rows, q.INW[1])
        return carry

    lax.fori_loop(0, 4, in_step, 0)
    halo_f = rcopy(q.PR.at[0:4, pl.ds(T, 8)], q.PR.at[pl.ds(k, 4), 0:8], q.halo.at[0], q.halo.at[1], mate)
    halo_ft = rcopy(q.PR.at[0:4, pl.ds(T, 8)], q.PR.at[pl.ds(1 - k, 4), 0:8], q.halo.at[0], q.halo.at[1], mate)
    halo_f.start()
    weight_start(3)
    swap_wait(2)
    ring_start(COT, (0, 1))
    swap_wait(1)
    halo_f.wait_send()
    halo_ft.wait_recv()

    def masks(s):
        reach = q.M[s].astype(F32)
        first = jnp.where(reach >= 1.0, 1.0, 0.0)
        second = jnp.where(reach >= 2.0, 1.0, 0.0)
        return jnp.concatenate([first, first], axis=1), jnp.concatenate([second, second], axis=1)

    def conv_step(s, carry):
        m1, m2 = masks(s)
        conv = q.ck[0:1, :] * q.PR[s, pl.ds(8, T)]
        conv = conv + q.ck[1:2, :] * q.PR[s, pl.ds(7, T)] * m1
        conv = conv + q.ck[2:3, :] * q.PR[s, pl.ds(6, T)] * m2
        q.CO[s] = conv
        q.GF[c, pl.ds(pl.multiple_of(s * T, T), T)] = (q.GCV[s] * conv).astype(BF)
        return carry

    lax.fori_loop(0, 2, conv_step, 0)
    ring_start(GF, (0, 3))
    lax.fori_loop(2, 4, conv_step, 0)
    ring_start(GF, (1, 2))
    ring_pass(OUX)
    ring_pass(GUX)
    ring_pass(GF)
    ring_start(COT, (2, 3))
    for d in (1, 3, 2):
        ring_take(OUX, d)
    out_core(k).start()
    weight_forward(3)
    for d in (1, 3, 2):
        ring_take(GUX, d)
    gu_core(k).start()
    for d in (1, 3, 2):
        ring_take(GF, d)
    out_ready()
    gu_ready()
    weight_ready(3)

    def out_step(n, carry):
        lanes = pl.ds(pl.multiple_of(n * HALF, HALF), HALF)
        gated = jnp.concatenate([q.GF[m] for m in range(4)], axis=1)
        branch = dot(gated, q.OUTF[:, :, :, :, lanes].reshape(D, HALF))
        q.HID[:, :, lanes] = q.XF[:, :, lanes].astype(F32) + branch.reshape(4, T, HALF)
        return carry

    lax.fori_loop(0, 2, out_step, 0)

    def norm_step(s, carry):
        hidden = q.HID[s]
        q.N2[s] = (hidden * norm_scale(hidden) * q.GA[1:2, :]).astype(BF)
        return carry

    lax.fori_loop(0, 4, norm_step, 0)

    COLS = ((0, 512), (512, 512), (1024, 128))
    for at, n in COLS:
        rows = q.N2[...].reshape(4 * T, D)
        gate = dot(rows, q.GUW[0, :, :, :, :, at : at + n].reshape(D, n))
        up = dot(rows, q.GUW[1, :, :, :, :, at : at + n].reshape(D, n))
        sig = 1.0 / (1.0 + jnp.exp(-gate))
        silu = gate * sig
        q.A[:, :, at : at + n] = (silu * up).astype(BF).reshape(4, T, n)
        q.GG[:, :, at : at + n] = (up * sig * (1.0 + gate * (1.0 - sig))).astype(BF).reshape(4, T, n)
        q.GG[:, :, H + at : H + at + n] = silu.astype(BF).reshape(4, T, n)
        if at == 0:
            ring_pass(COT)

    def unit(name):
        return next(u for u in UNITS if u[0] == name)

    def g(name, what):
        return getattr(q, name + "_" + what)

    def core_copy(name, core):
        return rcopy(g(name, "W").at[core], g(name, "C"), g(name, "s").at[7], g(name, "r").at[0], mate)

    def first_view(name, d, h):
        w = g(name, "W")
        if unit(name)[3] == 0:
            return w.at[k, pl.ds(2 * h, 2), mod(x + d, 4)]
        return w.at[k, slot_y(d), pl.ds(2 * h, 2)]

    def first_copy(name, n):
        e, h, d = ((2, 0, 1), (2, 1, 3), (1, 1, 1), (1, 0, 1), (3, 0, 3), (3, 1, 3))[n]
        if n < 2:
            dst = g(name, "T").at[h]
        else:
            dst = g(name, "R1").at[e // 2, pl.ds(2 * h, 2)]
        to = at_x(d) if unit(name)[3] == 0 else at_y(d)
        return rcopy(first_view(name, e, h), dst, g(name, "s").at[n], g(name, "r").at[1 + n], to)

    def second_copy(name, d):
        if unit(name)[3] == 0:
            src, to = g(name, "S").at[slot_y(d)], at_y(d)
        else:
            src, to = g(name, "S").at[mod(x + d, 4)], at_x(d)
        return rcopy(src, g(name, "R2").at[d - 1], g(name, "s").at[d - 1], g(name, "r").at[6 + d], to)

    def spread_x(name, d, place):
        view = g(name, "O").at[yhi, place]
        return rcopy(view, view, g(name, "s").at[d - 1], g(name, "r").at[9 + d], at_x(d))

    def ring_x(name):
        return Ring(name, lambda a, h: g(name, "O").at[h, a], x, at_x, 10)

    def spread_y(name, place):
        o = g(name, "O")
        view = o.at[place, x] if unit(name)[3] == 0 else o.at[place]
        return rcopy(view, view, g(name, "s").at[6], g(name, "r").at[16], at_y(2))

    def core_send(name):
        core_copy(name, 1 - k).start()

    def stage_one(name):
        core_copy(name, 1 - k).wait()
        w, other_part = g(name, "W"), g(name, "C")

        def add(i, carry):
            a, b = lax.div(i, 4), lax.rem(i, 4)
            w[k, a, b] = (w[k, a, b].astype(F32) + other_part[a, b].astype(F32)).astype(BF)
            return carry

        lax.fori_loop(0, 16, add, 0)
        for n in (0, 1, 2, 4):
            first_copy(name, n).start()

    def stage_pass(name):
        mid = g(name, "T")
        for n, e, h, last in ((0, 1, 0, 3), (1, 3, 1, 5)):
            first_copy(name, n).wait_recv()
            view = first_view(name, e, h)
            view[...] = (view[...].astype(F32) + mid[h].astype(F32)).astype(BF)
            first_copy(name, last).start()

    def stage_two(name):
        for n in (2, 4, 3, 5):
            first_copy(name, n).wait_recv()
        for n in range(6):
            first_copy(name, n).wait_send()
        w, got, total = g(name, "W"), g(name, "R1"), g(name, "S")

        def add(i, carry):
            mine = w[k, i, x] if unit(name)[3] == 0 else w[k, slot_y(0), i]
            total[i] = (mine.astype(F32) + got[0, i].astype(F32) + got[1, i].astype(F32)).astype(BF)
            return carry

        lax.fori_loop(0, 4, add, 0)
        for d in (1, 3, 2):
            second_copy(name, d).start()

    def stage_three(name):
        for d in (1, 3, 2):
            second_copy(name, d).wait()
        got, total = g(name, "R2"), g(name, "S")
        mine = total[slot_y(0)] if unit(name)[3] == 0 else total[x]
        g(name, "O")[yhi, x] = (mine.astype(F32) + got[0].astype(F32) + got[1].astype(F32) + got[2].astype(F32)).astype(BF)
        if unit(name)[3] == 0:
            spread_y(name, yhi).start()
        else:
            for d in (1, 3, 2):
                spread_x(name, d, x).start()

    def take_x(name):
        for d in (1, 3, 2):
            spread_x(name, d, x).wait_send()
            spread_x(name, d, mod(x - d, 4)).wait_recv()

    def take_y(name):
        spread_y(name, yhi).wait_send()
        spread_y(name, 1 - yhi).wait_recv()

    def stage_four(name):
        if unit(name)[3] == 0:
            take_y(name)
            ring_start(ring_x(name))
        else:
            take_x(name)
            spread_y(name, yhi).start()

    def stage_four_pass(name):
        if unit(name)[3] == 0:
            ring_pass(ring_x(name))

    def results(name, core):
        o = g(name, "O")
        half = unit(name)[3]
        if name in ("dn0", "dn1"):
            at = pl.multiple_of(core * W + half * 128, 128)
            return [(o, q.o_dn.at[:, :, :, pl.ds(at, 128)])]
        if name in ("gt", "up"):
            return [(o, q.o_gu.at[half, core])]
        if name == "oi0":
            at = pl.multiple_of(core * W, W)
            return [(o.at[:, :, :, 0:W], q.o_out.at[:, :, :, pl.ds(at, W)]), (o.at[:, :, :, W:], q.o_in.at[0, core])]
        return [(o.at[:, :, :, 0:W], q.o_in.at[1, core]), (o.at[:, :, :, W:], q.o_in.at[2, core])]

    def stage_five(name):
        if unit(name)[3] == 0:
            for d in (1, 3, 2):
                ring_take(ring_x(name), d)
            ring_end(ring_x(name))
        else:
            take_y(name)
        for n, (src, dst) in enumerate(results(name, k)):
            pltpu.make_async_copy(src, dst, g(name, "l").at[n]).start()
            rcopy(src, dst, g(name, "s").at[n], g(name, "r").at[17 + n], mate).start()

    def stage_six(name):
        for n, (src, dst) in enumerate(results(name, k)):
            pltpu.make_async_copy(src, dst, g(name, "l").at[n]).wait()
            rcopy(src, dst, g(name, "s").at[n], g(name, "r").at[17 + n], mate).wait_send()
        for n, (src, dst) in enumerate(results(name, 1 - k)):
            rcopy(src, dst, g(name, "s").at[n], g(name, "r").at[17 + n], mate).wait_recv()

    def features(ref, a, core):
        at = pl.multiple_of(a * HALF + core * W, W)
        return ref[:, :, pl.ds(at, W)].reshape(4 * T, W)

    def grad_down(core):
        both = jnp.concatenate([features(q.COT, a, core) for a in (0, 1)], axis=1)
        full = dot_tn(q.A[...].reshape(4 * T, H), both).astype(BF).reshape(2, 4, 144, 2 * W)
        for a in (0, 1):
            q.dn0_W[core, 2 * a : 2 * a + 2] = full[:, :, :, a * W : a * W + 128]
            q.dn1_W[core, 2 * a : 2 * a + 2] = full[:, :, :, a * W + 128 : (a + 1) * W]

    def grad_gate_up(core):
        def step(a, carry):
            rows = features(q.N2, a, core)
            q.gt_W[core, pl.ds(2 * a, 2)] = dot_tn(rows, q.GG[:, :, 0:H].reshape(4 * T, H)).astype(BF).reshape(2, 4, 32, H)
            q.up_W[core, pl.ds(2 * a, 2)] = dot_tn(rows, q.GG[:, :, H:].reshape(4 * T, H)).astype(BF).reshape(2, 4, 32, H)
            return carry

        lax.fori_loop(0, 2, step, 0)

    def grad_in(core):
        def step(a, carry):
            rows = features(q.N1, a, core)
            into = dot_tn(rows, q.GM[...].reshape(4 * T, 3 * W)).astype(BF).reshape(2, 4, 32, 3 * W)
            q.oi0_W[core, pl.ds(2 * a, 2), :, :, W:] = into[:, :, :, 0:W]
            q.oi1_W[core, pl.ds(2 * a, 2)] = into[:, :, :, W:]
            return carry

        lax.fori_loop(0, 2, step, 0)

    def grad_out(core):
        both = jnp.concatenate([features(q.GB, a, core) for a in (0, 1)], axis=1)
        full = dot_tn(q.GF[c], both).astype(BF).reshape(2, 4, 32, 2 * W)
        for a in (0, 1):
            q.oi0_W[core, 2 * a : 2 * a + 2, :, :, 0:W] = full[:, :, :, a * W : (a + 1) * W]

    def out_pair(pair):
        put_pair("RF", q.OWNF, pair, dot(two_chunks(q.A, pair), q.DNW[...]))

    for d in (1, 3, 2):
        ring_take(COT, d)
    for at, n in COLS:
        ga = dot_nt(q.COT[...].reshape(4 * T, D), q.DNW[at : at + n, :]).reshape(4, T, n)
        for first in (0, H):
            lanes = slice(first + at, first + at + n)
            q.GG[:, :, lanes] = (ga * q.GG[:, :, lanes].astype(F32)).astype(BF)

    def back_pair(pair):
        gate = dot_nt(two_chunks(q.GG, pair, slice(0, H)), q.GUW[0].reshape(D, H))
        up = dot_nt(two_chunks(q.GG, pair, slice(H, 2 * H)), q.GUW[1].reshape(D, H))
        put_pair("R2", q.OWN, pair, gate + up)

    back_pair((2, 0))
    grad_gate_up(1 - k)
    core_send("gt")
    core_send("up")
    back_pair((1, 3))
    grad_gate_up(k)
    stage_one("gt")
    stage_one("up")
    out_pair((2, 0))
    for ring in (XF, GF, COT):
        ring_end(ring)
    grad_down(1 - k)
    core_send("dn0")
    core_send("dn1")
    grad_down(k)
    stage_one("dn0")
    stage_one("dn1")

    def norm_back(value, scale, gain, grad):
        weighted = grad * gain
        inner = jnp.sum(weighted * value, axis=1, keepdims=True)
        back = scale * weighted - value * (scale * scale * scale) * inner / D
        return back, jnp.sum(grad * value * scale, axis=0, keepdims=True)

    grad_normed = reduce_sum("R2", q.OWN)
    hidden = q.HID[c]
    back, grad_gain = norm_back(hidden, norm_scale(hidden), q.GA[1:2, :], grad_normed)
    q.SM[...] = jnp.zeros((8, D), F32)
    q.SM[1:2, :] = grad_gain
    grad_hidden = q.COT[c].astype(F32) + back
    q.GB[c] = grad_hidden.astype(BF)
    q.OWN[...] = grad_hidden
    grad_gated = dot_nt(q.GB[c], q.OUTF[...].reshape(D, D)).astype(BF)
    for n in range(4):
        q.GGS[n] = grad_gated[:, n * W : (n + 1) * W]

    def gated_copy(d, dst):
        return rcopy(q.GGS.at[mod(c + d, 4)], q.GGR.at[dst], q.GG_s.at[d], q.GG_r.at[d], at_z(d))

    for d in (1, 3, 2):
        gated_copy(d, c).start()
    q.GGR[c] = q.GGS[c]
    stage_pass("gt")
    stage_pass("up")

    def home(n):
        buf, out = ((q.MIXB, q.o_mixed), (q.GTB, q.o_gt))[n]
        base = 6 + 2 * n
        halves = lambda a: buf.at[:, pl.ds(pl.multiple_of(a * HALF, HALF), HALF)]
        rows = lambda j: out.at[pl.ds(j * T, T), :]
        near_local = pltpu.make_async_copy(halves(r), rows(k), q.sw_r.at[base])
        near_far = rcopy(halves(r), rows(k), q.sw_s.at[base], q.sw_r.at[base + 1], mate)
        away = rcopy(halves(1 - r), rows(k), q.sw_s.at[base + 1], q.sw_r.at[base + k], dev(r_=1 - r, k_=r))
        return halves, rows, base, near_local, near_far, away

    def home_start(n):
        halves, rows, base, near_local, near_far, away = home(n)

        @pl.when(same)
        def _():
            near_local.start()

        @pl.when(other)
        def _():
            near_far.start()

        away.start()

    def home_wait(n):
        halves, rows, base, near_local, near_far, away = home(n)

        @pl.when(same)
        def _():
            near_local.wait()
            rcopy(halves(r), rows(1 - k), q.sw_s.at[base], q.sw_r.at[base + 1], mate).wait_recv()

        @pl.when(other)
        def _():
            near_far.wait_send()
            for j in (0, 1):
                rcopy(halves(r), rows(j), q.sw_s.at[base], q.sw_r.at[base + j], dev(r_=1 - r)).wait_recv()

        away.wait_send()

    @pl.when(k == 1)
    def _():
        q.FM[0, 4, pl.ds(T, 8)] = jnp.zeros((8, W), F32)
        q.FM[1, 4, pl.ds(T, 8)] = jnp.zeros((8, W), F32)

    for d in (1, 3, 2):
        gated_copy(d, c).wait_send()
        gated_copy(d, mod(c - d, 4)).wait_recv()
    ring_start(GB)

    def conv_back_step(s, carry):
        grad_gated = q.GGR[s].astype(F32)
        q.GM[s, :, W : 2 * W] = (grad_gated * q.CO[s]).astype(BF)
        grad_conv = grad_gated * q.GCV[s]
        q.GCONV[s] = grad_conv
        m1, m2 = masks(s)
        q.FM[0, s + 1, 0:T] = grad_conv * m1
        q.FM[1, s + 1, 0:T] = grad_conv * m2
        return carry

    lax.fori_loop(0, 4, conv_back_step, 0)
    halo_b = rcopy(q.FM.at[:, 1:5, 0:8], q.FM.at[:, pl.ds(k, 4), pl.ds(T, 8)], q.halo.at[2], q.halo.at[3], mate)
    halo_bt = rcopy(q.FM.at[:, 1:5, 0:8], q.FM.at[:, pl.ds(1 - k, 4), pl.ds(T, 8)], q.halo.at[2], q.halo.at[3], mate)
    halo_b.start()
    stage_pass("dn0")
    stage_pass("dn1")
    halo_b.wait_send()
    halo_bt.wait_recv()

    def product_back_step(s, carry):
        grad_conv = q.GCONV[s]
        grad_product = q.ck[0:1, :] * grad_conv
        grad_product = grad_product + q.ck[1:2, :] * q.FM[0, s + 1, pl.ds(1, T)]
        grad_product = grad_product + q.ck[2:3, :] * q.FM[1, s + 1, pl.ds(2, T)]
        q.SM[2:3, 0:W] += jnp.sum(grad_conv * q.PR[s, pl.ds(8, T)], axis=0, keepdims=True)
        q.SM[3:4, 0:W] += jnp.sum(q.FM[0, s + 1, pl.ds(0, T)] * q.PR[s, pl.ds(7, T)], axis=0, keepdims=True)
        q.SM[4:5, 0:W] += jnp.sum(q.FM[1, s + 1, pl.ds(0, T)] * q.PR[s, pl.ds(6, T)], axis=0, keepdims=True)
        q.GM[s, :, 0:W] = (grad_product * q.VAL[s]).astype(BF)
        q.GM[s, :, 2 * W :] = (grad_product * q.GBV[s]).astype(BF)
        return carry

    lax.fori_loop(0, 4, product_back_step, 0)

    def in_pair(pair):
        part = [dot_nt(two_chunks(q.GM, pair, slice(n * W, (n + 1) * W)), q.INW[n]) for n in range(3)]
        put_pair("R3", q.OWNB, pair, part[0] + part[1] + part[2])

    class Small:
        def __init__(self, name):
            self.name = name
            self.own, self.other = getattr(q, name), getattr(q, name + "C")
            self.axes = [(getattr(q, name + axis), me, at) for axis, me, at in (("X", x, at_x), ("Y", y, at_y), ("Z", c, at_z))]
            self.sends, self.takes = getattr(q, name + "_s"), getattr(q, name + "_r")

        def core(self):
            return rcopy(self.own, self.other, self.sends.at[9], self.takes.at[9], mate)

        def copy(self, n, d, a):
            buf, _, to = self.axes[n]
            return rcopy(buf.at[a], buf.at[a], self.sends.at[3 * n + d - 1], self.takes.at[3 * n + d - 1], to(d))

        def take(self, n):
            buf, me, _ = self.axes[n]
            for d in (1, 2, 3):
                self.copy(n, d, me).wait_send()
                self.copy(n, d, mod(me - d, 4)).wait_recv()
            return (buf[0] + buf[1]) + (buf[2] + buf[3])

        def step(self, n):
            if n == 0:
                self.core().wait()
                value = self.own[...] + self.other[...]
            else:
                value = self.take(n - 1)
            self.own[...] = value
            buf, me, _ = self.axes[n]
            buf[me] = value
            for d in (1, 2, 3):
                self.copy(n, d, me).start()

    early, late = Small("SE"), Small("SL")
    for n in range(8):
        q.SE[n : n + 1, :] = q.SM[1:2, n * 128 : (n + 1) * 128]
    for n in range(8):
        q.SE[8 + n : 9 + n, :] = q.SM[2 + n // 2 : 3 + n // 2, (n % 2) * 128 : (n % 2 + 1) * 128]
    early.core().start()
    ring_pass(GB)
    stage_two("gt")
    stage_two("up")
    grad_in(1 - k)
    core_send("oi1")
    in_pair((2, 0))
    stage_two("dn0")
    stage_two("dn1")
    grad_in(k)
    stage_one("oi1")
    for d in (1, 3, 2):
        ring_take(GB, d)
    grad_out(1 - k)
    core_send("oi0")
    in_pair((1, 3))
    stage_three("gt")
    stage_three("up")
    grad_out(k)
    stage_one("oi0")
    ring_end(GB)
    early.step(0)
    stage_pass("oi1")
    out_pair((1, 3))
    stage_three("dn0")
    stage_three("dn1")
    stage_four("gt")
    stage_four("up")
    stage_pass("oi0")
    early.step(1)
    stage_two("oi1")
    grad_normed = reduce_sum("R3", q.OWNB)
    inputs = q.XF[c].astype(F32)
    back, grad_gain = norm_back(inputs, norm_scale(inputs), q.GA[0:1, :], grad_normed)
    for n in range(8):
        q.SL[n : n + 1, :] = grad_gain[:, n * 128 : (n + 1) * 128]
    late.core().start()
    q.GTB[...] = (q.OWN[...] + back).astype(BF)
    home_start(1)
    stage_two("oi0")
    stage_four_pass("gt")
    stage_four("dn0")
    stage_four("dn1")
    stage_three("oi1")
    stage_three("oi0")
    late.step(0)
    early.step(2)
    stage_four_pass("dn0")
    stage_four("oi1")
    stage_four("oi0")
    late.step(1)
    stage_five("gt")
    stage_five("up")
    stage_four_pass("oi0")
    late.step(2)
    q.MIXB[...] = (q.HID[c] + reduce_sum("RF", q.OWNF)).astype(BF)
    home_start(0)
    stage_five("dn0")
    stage_five("dn1")
    early_gain = early.take(2)
    late_gain = late.take(2)
    q.SL[...] = late_gain
    q.SEC[0:8, :] = early_gain[0:8, :]
    q.o_small[...] = jnp.zeros((8, HALF), F32)
    for n in range(4):
        lanes = slice(n * 128, (n + 1) * 128)
        q.o_small[0:1, lanes] = q.SL[pl.ds(r * 4 + n, 1), :]
        q.o_small[1:2, lanes] = q.SEC[pl.ds(r * 4 + n, 1), :]
    for n in range(6):
        q.o_small[2 + n // 2 : 3 + n // 2, (n % 2) * 128 : (n % 2 + 1) * 128] = q.SE[8 + n : 9 + n, :]
    stage_five("oi0")
    stage_five("oi1")
    home_wait(0)
    home_wait(1)
    gain_send.wait_send()
    for w in (0, 3):
        weight_end(w)
    for name in ("dn0", "dn1", "gt", "up", "oi0", "oi1"):
        stage_six(name)


def cast_kernel(mixed, tokens, small, g_in, g_out, g_gu, g_dn, o_mixed, o_tokens, o_mixer, o_kernel, o_ffn, o_in, o_out, o_gu, o_dn):
    o_mixed[...] = mixed[...]
    o_mixer[...] = small[0:1, :]
    o_ffn[...] = small[1:2, :]
    o_kernel[...] = small[2:5, 0:W]
    for src, dst in ((tokens, o_tokens), (g_in, o_in), (g_out, o_out), (g_gu, o_gu), (g_dn, o_dn)):
        dst[...] = src[...].astype(F32)


def cast_all(*arrays):
    steps = 4

    def cut(shape):
        at = len(shape) - 2
        block = shape[:at] + (shape[at] // steps, shape[-1])
        return pl.BlockSpec(block, lambda i: (0,) * at + (i, 0))

    def whole(shape):
        return pl.BlockSpec(shape, lambda i: (0, 0))

    specs = [whole(a.shape) if n == 2 else cut(a.shape) for n, a in enumerate(arrays)]
    small = [(1, HALF), (3, W), (1, HALF)]
    kinds = [BF] + [F32] * 5
    big = [cut(a.shape) for n, a in enumerate(arrays) if n != 2]
    shapes = [jax.ShapeDtypeStruct(a.shape, kind) for a, kind in zip([a for n, a in enumerate(arrays) if n != 2], kinds)]
    return pl.pallas_call(
        cast_kernel,
        grid=(steps,),
        in_specs=specs,
        out_specs=big[:2] + [whole(n) for n in small] + big[2:],
        out_shape=shapes[:2] + [jax.ShapeDtypeStruct(n, F32) for n in small] + shapes[2:],
        compiler_params=pltpu.CompilerParams(vmem_limit_bytes=60 * 2**20),
        name="cast_all",
    )(*arrays)


def per_device(
    tokens,
    mixer_gain,
    in_weight,
    conv_kernel,
    out_weight,
    ffn_gain,
    gate_up_weight,
    down_weight,
    conv_reach,
    cotangent,
):
    hbm = pl.BlockSpec(memory_space=pl.ANY)
    vmem = pl.BlockSpec(memory_space=pltpu.VMEM)
    mixed, grad_tokens, small, g_in, g_out, g_gu, g_dn = pl.pallas_call(
        kernel,
        out_shape=(
            jax.ShapeDtypeStruct((2 * T, HALF), BF),
            jax.ShapeDtypeStruct((2 * T, HALF), BF),
            jax.ShapeDtypeStruct((8, HALF), F32),
            jax.ShapeDtypeStruct((3, 2, 2, 4, 32, W), BF),
            jax.ShapeDtypeStruct((2, 4, 32, HALF), BF),
            jax.ShapeDtypeStruct((2, 2, 2, 4, 32, H), BF),
            jax.ShapeDtypeStruct((2, 4, 144, HALF), BF),
        ),
        in_specs=[hbm, hbm, vmem, vmem, vmem, vmem, hbm, hbm, hbm, hbm],
        out_specs=(hbm, hbm, vmem, hbm, hbm, hbm, hbm),
        scratch_shapes=list(scratch_list().values()),
        compiler_params=pltpu.CompilerParams(
            collective_id=0, has_side_effects=True, vmem_limit_bytes=60 * 2**20
        ),
        name="block_step",
    )(
        tokens,
        cotangent,
        conv_reach.reshape(4, T),
        mixer_gain.reshape(1, HALF),
        ffn_gain.reshape(1, HALF),
        conv_kernel,
        in_weight,
        out_weight,
        gate_up_weight.reshape(2, 4, 2, 64, H),
        down_weight,
    )
    results = cast_all(
        mixed,
        grad_tokens,
        small,
        g_in.reshape(3, HALF, W),
        g_out.reshape(W, HALF),
        g_gu.reshape(2, HALF, H),
        g_dn.reshape(H, HALF),
    )
    mixed, grad_tokens, mixer, kernel_grad, ffn, g_in, g_out, g_gu, g_dn = results
    return (mixed, grad_tokens, mixer.reshape(HALF), g_in, kernel_grad, g_out, ffn.reshape(HALF), g_gu, g_dn)


def solution(mesh):
    return jax.shard_map(
        per_device,
        mesh=mesh,
        in_specs=(
            P(("dp", "col"), "row"),
            P("row"),
            P(None, "row", "col"),
            P(None, "col"),
            P("col", "row"),
            P("row"),
            P(None, "row", "col"),
            P("col", "row"),
            P(("dp", "row")),
            P(("dp", "col"), "row"),
        ),
        out_specs=(
            P(("dp", "col"), "row"),
            P(("dp", "col"), "row"),
            P("row"),
            P(None, "row", "col"),
            P(None, "col"),
            P("col", "row"),
            P("row"),
            P(None, "row", "col"),
            P("col", "row"),
        ),
        check_vma=False,
    )
```
